256 devices in a mesh: lines: 32 (over x, z), slab: 8 (over y, core).
Axes of the slice: x: 4, y: 4, z: 8, core: 2. Of those that a mesh axis runs over, the one named last changes fastest.
Arguments:
- fields: float32 [6, 2097152], P(None, ('lines', 'slab')), may hold values from -6 to 6
- frac_x: float32 [2097152], P(('lines', 'slab')), may hold values from 0 to 1
- owner: int32 [2097152], P(('lines', 'slab')), may hold values from 0 to 31, as said below
- slab: int32 [2097152], P(('lines', 'slab')), may hold values from 0 to 7
- line_in: int32 [2097152], P(('lines', 'slab')), may hold values from 0 to 63
- xcell: int32 [2097152], P(('lines', 'slab')), may hold values from 0 to 511, as said below
- tile_count: int32 [16384], P(('lines', 'slab')), may hold values from 64 to 128, as said below
- y_offset: int32 [512, 64, 256], P('lines', 'slab'), may hold values from -2 to 2
- y_frac: float32 [512, 64, 256], P('lines', 'slab'), may hold values from 0 to 1
Outputs:
- remeshed: float32 [6, 512, 64, 256], P(None, 'lines', 'slab')
The draws below stay inside these ranges and needn't reach their ends.
Inputs may be any that keep to these rules, and one draw needn't show every extreme that they name: Tile t of a device holds its live particles in the first tile_count[t] of its 128 slots; the other slots are empty and whatever they hold is ignored. The first tile of every device is full. Among the live particles of one device at most 48 share one pair of owner and slab, and in every draw one such pair holds exactly 48 of them. Among the live particles of one device at most 48 share one pair of x range (xcell div 16) and slab, and in every draw one such pair holds exactly 48 of them.
All inputs are finite; a program needn't handle non-finite values.
Results may differ from the reference program's by a relative error of at most 0.00002.
Values sent between devices are 32-bit elements; how exact they have to be, the bound alone decides.
No kernel may reach another device: no remote copies, remote signals or barrier semaphores. Data moves between devices by JAX's collectives and lax.ppermute only.
A program may use at most 128 MiB of HBM per device.

```python
import jax
import jax.numpy as jnp
from jax import lax

FIELDS = 6
NX = 512
NY = 256
ZS = 8
TILE = 128
TILES_DEV = 64
NZ = 64
XL = 16
YL = 8
P_DEV = 8192
PARTICLES = 2097152
CAP = 48
N_LINES = 32
N_SLAB = 8


def shared_layout(key):
    devices_all = N_LINES * N_SLAB
    key_counts, key_order, key_busy, key_shuffle = jax.random.split(jax.random.fold_in(key, 7), 4)
    counts = jax.random.randint(key_counts, (devices_all, TILES_DEV), TILE // 2, TILE + 1).astype(jnp.int32)
    counts = counts.at[:, 0].set(TILE)
    slot_in_tile = jnp.arange(P_DEV, dtype=jnp.int32) % TILE
    alive_slot = (slot_in_tile[None, :] < jnp.repeat(counts, TILE, axis=1)).astype(jnp.int32)
    order_keys = jax.random.split(key_order, devices_all)
    sort_order = jax.vmap(lambda one_key: jax.random.permutation(one_key, P_DEV))(order_keys).astype(jnp.int32)
    ranked = jnp.cumsum(jnp.take_along_axis(alive_slot, sort_order, axis=1), axis=1) - 1
    busiest = jax.random.randint(key_busy, (devices_all, 1), 0, devices_all).astype(jnp.int32)
    others = (busiest + 1 + jnp.maximum(ranked - CAP, 0) % (devices_all - 1)) % devices_all
    pair_sorted = jnp.where(ranked < CAP, busiest, others).astype(jnp.int32)
    device_rows = jnp.arange(devices_all, dtype=jnp.int32)[:, None]
    pair_index = jnp.zeros((devices_all, P_DEV), jnp.int32).at[device_rows, sort_order].set(pair_sorted)
    shuffle_keys = jax.random.split(key_shuffle, devices_all)
    shuffle = jax.vmap(lambda one_key: jax.random.permutation(one_key, N_LINES))(shuffle_keys).astype(jnp.int32)
    return (counts, pair_index, shuffle)


def draw_tile_count(key, part):
    counts, pair_index, shuffle = shared_layout(key)
    return counts.reshape(-1)


def draw_owner(key, part):
    counts, pair_index, shuffle = shared_layout(key)
    return (pair_index // N_SLAB).reshape(-1).astype(jnp.int32)


def draw_slab(key, part):
    counts, pair_index, shuffle = shared_layout(key)
    return (pair_index % N_SLAB).reshape(-1).astype(jnp.int32)


def draw_xcell(key, part):
    counts, pair_index, shuffle = shared_layout(key)
    key = jax.random.fold_in(key, 4)
    line_owner = pair_index // N_SLAB
    x_range = jnp.take_along_axis(shuffle, line_owner, axis=1)
    inside = jax.random.randint(key, line_owner.shape, 0, XL).astype(jnp.int32)
    return (x_range * XL + inside).reshape(-1).astype(jnp.int32)


def set_ends(drawn, rng, smallest, largest):
    place = [jax.random.randint(jax.random.fold_in(rng, axis), (), 0, length) for axis, length in enumerate(drawn.shape)]
    main_axis = drawn.shape.index(max(drawn.shape))
    neighbour = place[:main_axis] + [(place[main_axis] + 1) % drawn.shape[main_axis]] + place[main_axis + 1:]
    return drawn.at[tuple(place)].set(smallest).at[tuple(neighbour)].set(largest)


def level_of(key, dims, shards, smallest, high):
    loudness = 1.0
    for axis_at, shards_of in shards:
        draws = jax.random.uniform(jax.random.fold_in(jax.random.fold_in(key, 6), axis_at), (shards_of,), jnp.float32, smallest / len(shards), high / len(shards))
        loudness = loudness * jnp.repeat(jnp.exp(draws), dims[axis_at] // shards_of).reshape((-1,) + (1,) * (len(dims) - 1 - axis_at))
    return loudness


def centred(stream_key, extent, width, most, pieces=(), kind=jnp.bfloat16):
    loudness = level_of(stream_key, extent, pieces, -0.22, 0.18) if pieces else 1.0
    drawn = jax.random.normal(stream_key, extent, jnp.float32) * width * loudness
    return jnp.minimum(jnp.maximum(drawn, -most), most).astype(kind)


def setup_inputs(seed: int = 0) -> dict:
    key_list = jax.random.split(jax.random.key(seed), 10)
    fields = centred(key_list[0], (FIELDS, PARTICLES), 1.0, 6.0, ((1, 256),), jnp.float32)
    frac_x = jnp.clip(1.0 * jax.random.uniform(key_list[1], (PARTICLES,), jnp.float32) ** level_of(key_list[1], (PARTICLES,), ((0, 256),), -0.2, 0.2), 0.0, 1.0)
    owner = draw_owner(jax.random.fold_in(key_list[9], 71), 0)
    slab = draw_slab(jax.random.fold_in(key_list[9], 71), 0)
    line_in = set_ends(jax.random.randint(key_list[4], (PARTICLES,), 0, YL * ZS), jax.random.fold_in(key_list[4], 1), 0, (YL * ZS) - 1).astype(jnp.int32)
    xcell = draw_xcell(jax.random.fold_in(key_list[9], 71), 0)
    tile_count = draw_tile_count(jax.random.fold_in(key_list[9], 71), 0)
    y_offset = set_ends(jax.random.randint(key_list[7], (NX, NZ, NY), -2, 3), jax.random.fold_in(key_list[7], 1), -2, 2).astype(jnp.int32)
    y_frac = jnp.clip(1.0 * jax.random.uniform(key_list[8], (NX, NZ, NY), jnp.float32) ** level_of(key_list[8], (NX, NZ, NY), ((0, 32), (1, 8)), -0.2, 0.2), 0.0, 1.0)
    return {"fields": fields, "frac_x": frac_x, "owner": owner, "slab": slab, "line_in": line_in, "xcell": xcell, "tile_count": tile_count, "y_offset": y_offset, "y_frac": y_frac}


def kernel_weights(offset):
    remain = 1.0 - offset
    return (-0.5 * offset * remain * remain,
            1.0 - 2.5 * offset * offset + 1.5 * offset * offset * offset,
            1.0 - 2.5 * remain * remain + 1.5 * remain * remain * remain,
            -0.5 * offset * offset * remain)


def reference(fields, frac_x, owner, slab, line_in, xcell, tile_count, y_offset, y_frac):
    position = jnp.arange(PARTICLES, dtype=jnp.int32)
    alive_slot = (position % TILE) < tile_count[position // TILE]
    live_mask = jnp.where(alive_slot, 1.0, 0.0).astype(jnp.float32)
    y_pos = owner * YL + line_in // ZS
    z_pos = slab * ZS + line_in % ZS
    weights_x = kernel_weights(frac_x)
    x_index = [(((xcell + neighbor) % NX) * NZ + z_pos) * NY + y_pos for neighbor in (-1, 0, 1, 2)]
    lattice_node = jnp.arange(NX * NZ * NY, dtype=jnp.int32)
    y_node = lattice_node % NY
    shift_cells = y_offset.reshape(-1)
    weights_y = kernel_weights(y_frac.reshape(-1))
    y_index = [lattice_node - y_node + (y_node + shift_cells + neighbor) % NY for neighbor in (-1, 0, 1, 2)]

    def one_field(values):
        values = values * live_mask
        lattice = jnp.zeros((NX * NZ * NY,), jnp.float32)
        for count in range(4):
            lattice = lattice.at[x_index[count]].add(values * weights_x[count])
        result = jnp.zeros((NX * NZ * NY,), jnp.float32)
        for count in range(4):
            result = result.at[y_index[count]].add(lattice * weights_y[count])
        return result.reshape(NX, NZ, NY)

    return lax.map(one_field, fields)
```

```python
import functools

import jax
import jax.numpy as jnp
from jax import lax
from jax.experimental import pallas as pl
from jax.experimental.pallas import tpu as pltpu
from jax.sharding import PartitionSpec as P

F32 = jnp.float32
BF16 = jnp.bfloat16
NT = (((1,), (1,)), ((), ()))

FIELDS = 6
SLOTS = 48
VALUES = 8
PEERS = 256
CHUNK = 256


def kernel_weights(offset):
    remain = 1.0 - offset
    return (
        -0.5 * offset * remain * remain,
        1.0 - 2.5 * offset * offset + 1.5 * offset * offset * offset,
        1.0 - 2.5 * remain * remain + 1.5 * remain * remain * remain,
        -0.5 * offset * offset * remain,
    )


def split(value):
    high = value.astype(BF16).astype(F32)
    return high, (value - high).astype(BF16).astype(F32)


def bucket_kernel(fields, frac, owner, slab, line_in, xcell, count, out, key_s, rank_s, place_s, upper_s, acc):
    rows = key_s.shape[0]
    lane = lax.broadcasted_iota(jnp.int32, key_s.shape, 1)
    alive = lane < count[...]
    key = (xcell[...] >> 4) * 8 + slab[...]
    key_s[...] = jnp.where(alive, key, -1).astype(F32)
    place_s[0] = (owner[...] * 8 + (line_in[...] >> 3)).astype(F32)
    place_s[1] = ((((line_in[...] & 7) * 16) + (xcell[...] & 15)) * 256).astype(F32)
    place_s[2], place_s[3] = split(frac[...])
    before = lax.broadcasted_iota(jnp.int32, (CHUNK, CHUNK), 0) < lax.broadcasted_iota(jnp.int32, (CHUNK, CHUNK), 1)
    upper_s[...] = jnp.where(before, 1.0, 0.0).astype(BF16)
    peer = lax.broadcasted_iota(jnp.int32, (PEERS, 128), 0).astype(F32)

    def row_of(ref, row):
        return ref[pl.ds(row, 1), :]

    def hits(row):
        return row_of(key_s, row) == peer

    unroll = 4

    def rank_step(step, base):
        for part in range(unroll):
            row = (step * unroll + part) * 2
            hit = [hits(row + half) for half in range(2)]
            one = jnp.concatenate([jnp.where(h, 1.0, 0.0).astype(BF16) for h in hit], axis=1)
            earlier = jnp.dot(one, upper_s[...], preferred_element_type=F32)
            for half in range(2):
                seen = earlier[:, half * 128:(half + 1) * 128] + base
                rank_s[pl.ds(row + half, 1), :] = jnp.sum(jnp.where(hit[half], seen, 0.0), axis=0, keepdims=True)
            base = base + jnp.dot(one, jnp.ones((CHUNK, 128), BF16), preferred_element_type=F32)
        return base

    lax.fori_loop(0, rows // (2 * unroll), rank_step, jnp.zeros((PEERS, 128), F32))

    slot = lax.broadcasted_iota(jnp.int32, (SLOTS, 128), 0).astype(F32)
    wide = 8
    acc[...] = jnp.zeros_like(acc)

    def send_step(step, carry):
        ones, packed = [], []
        for part in range(wide):
            row = step * wide + part
            ones.append(jnp.where(hits(row), 1.0, 0.0).astype(BF16))
            here = row_of(rank_s, row) == slot
            block = fields[:, pl.ds(pl.multiple_of(row * 128, 128), 128)]
            high, low = split(block)
            highs = [high[f:f + 1] for f in range(FIELDS)]
            lows = [low[f:f + 1] for f in range(FIELDS)]
            highs += [place_s[2, pl.ds(row, 1), :], place_s[0, pl.ds(row, 1), :]]
            lows += [place_s[3, pl.ds(row, 1), :], place_s[1, pl.ds(row, 1), :]]
            packed.append(jnp.concatenate([jnp.where(here, v, 0.0).astype(BF16) for v in highs + lows], axis=0))
        acc[...] += lax.dot_general(
            jnp.concatenate(packed, axis=1), jnp.concatenate(ones, axis=1), NT, preferred_element_type=F32
        )
        return carry

    lax.fori_loop(0, rows // wide, send_step, 0)
    half = VALUES * SLOTS
    total = acc[:half, :] + acc[half:, :]
    out[...] = jnp.swapaxes(total, 0, 1)[:, None, :]


def deposit_kernel(arrived, lattice, low_edge, high_edge, flat_s, weight_s, xin_s, yat_s, zat_s, acc):
    flat_s[...] = jnp.swapaxes(arrived[:, 0, :], 0, 1)
    offset = flat_s[6 * SLOTS:7 * SLOTS, :]
    place = flat_s[7 * SLOTS:8 * SLOTS, :].astype(jnp.int32)
    for number, weight in enumerate(kernel_weights(offset)):
        weight_s[number] = weight
    yat_s[...] = (place & 255).astype(F32)
    xin_s[...] = ((place >> 8) & 15).astype(F32)
    zat_s[...] = (place >> 12).astype(F32)
    acc[...] = jnp.zeros_like(acc)
    sub = lax.broadcasted_iota(jnp.int32, (8, PEERS), 0)
    low_rows = (sub + 1).astype(F32)
    high_rows = (sub + 9).astype(F32)
    edge_rows = jnp.where(sub % 4 == 0, 0, jnp.where(sub % 4 == 3, 99, 16 + sub % 4)).astype(F32)
    first = sub < 4
    y_iota = lax.broadcasted_iota(jnp.int32, (256, PEERS), 0).astype(F32)
    per = 2

    def step(index, carry):
        packed, y_rows, z_rows = [], [], []
        for part in range(per):
            slot = index * per + part
            weights = [weight_s[k, pl.ds(slot, 1), :] for k in range(4)]
            xin = xin_s[pl.ds(slot, 1), :]
            spread = []
            for nodes in (low_rows, high_rows, edge_rows):
                apart = nodes - xin
                value = jnp.zeros((8, PEERS), F32)
                for k in range(4):
                    value = jnp.where(apart == float(k), weights[k], value)
                spread.append(value)
            field = [flat_s[pl.ds(f * SLOTS + slot, 1), :] for f in range(FIELDS)]
            groups = []
            for f in range(FIELDS):
                groups += [spread[0] * field[f], spread[1] * field[f]]
            for f in range(0, FIELDS, 2):
                groups.append(spread[2] * jnp.where(first, field[f], field[f + 1]))
            groups.append(jnp.zeros((8, PEERS), F32))
            whole = jnp.concatenate(groups, axis=0)
            high = whole.astype(BF16)
            low = (whole - high.astype(F32)).astype(BF16)
            packed.append(jnp.concatenate([high, low], axis=0))
            y_rows.append(yat_s[pl.ds(slot, 1), :])
            z_rows.append(zat_s[pl.ds(slot, 1), :])
        values = jnp.concatenate(packed, axis=1)
        for z in range(8):
            one = jnp.concatenate(
                [
                    jnp.where(jnp.where(z_rows[part] == float(z), y_rows[part], -1.0) == y_iota, 1.0, 0.0).astype(BF16)
                    for part in range(per)
                ],
                axis=1,
            )
            acc[z] += lax.dot_general(one, values, NT, preferred_element_type=F32)
        return carry

    lax.fori_loop(0, SLOTS // per, step, 0)
    for z in range(8):
        nodes = jnp.swapaxes(acc[z, :, :128] + acc[z, :, 128:], 0, 1)
        for f in range(FIELDS):
            for half in range(2):
                at = (f * 2 + half) * 8
                lattice[f, half * 8:half * 8 + 8, z, :] = nodes[at:at + 8, :]
            at = 96 + f * 4
            low_edge[f, 0, z:z + 1, :] = nodes[at:at + 1, :]
            high_edge[f, 0, z:z + 1, :] = nodes[at + 1:at + 2, :]
            high_edge[f, 1, z:z + 1, :] = nodes[at + 2:at + 3, :]


def y_kernel(lattice, from_right, from_left, y_offset, y_frac, out):
    width = y_offset.shape[0]

    def one_x(x, halo):
        weights = kernel_weights(y_frac[x])
        shift = y_offset[x]
        is_shift = [shift == s for s in range(-2, 3)]
        factors = []
        for travel in range(-3, 5):
            factor = jnp.zeros_like(weights[0])
            for s in range(-2, 3):
                if -1 <= travel - s <= 2:
                    factor = jnp.where(is_shift[s + 2], weights[travel - s + 1], factor)
            factors.append(factor)
        for f in range(FIELDS):
            values = lattice[f, x]
            if halo is not None:
                values = values + halo[0][f, halo[1]]
            total = values * factors[3]
            for travel in range(-3, 5):
                if travel:
                    total = total + pltpu.roll(values * factors[travel + 3], travel % values.shape[1], 1)
            out[f, x] = total

    one_x(0, (from_left, 0))
    one_x(1, (from_left, 1))
    one_x(width - 1, (from_right, 0))

    def body(x, carry):
        one_x(x, None)
        return carry

    lax.fori_loop(2, width - 1, body, 0)


def params(mib):
    return pltpu.CompilerParams(vmem_limit_bytes=mib << 20)


def bucket(fields, frac, owner, slab, line_in, xcell, count):
    rows = frac.shape[0] // 128
    grid2 = lambda v: v.reshape(rows, 128)
    return pl.pallas_call(
        bucket_kernel,
        out_shape=jax.ShapeDtypeStruct((PEERS, 1, VALUES * SLOTS), F32),
        scratch_shapes=[
            pltpu.VMEM((rows, 128), F32),
            pltpu.VMEM((rows, 128), F32),
            pltpu.VMEM((4, rows, 128), F32),
            pltpu.VMEM((CHUNK, CHUNK), BF16),
            pltpu.VMEM((2 * VALUES * SLOTS, PEERS), F32),
        ],
        compiler_params=params(24),
        name="bucket",
    )(fields, grid2(frac), grid2(owner), grid2(slab), grid2(line_in), grid2(xcell), count.reshape(rows, 1))


def deposit(arrived):
    return pl.pallas_call(
        deposit_kernel,
        out_shape=(
            jax.ShapeDtypeStruct((FIELDS, 16, 8, 256), F32),
            jax.ShapeDtypeStruct((FIELDS, 1, 8, 256), F32),
            jax.ShapeDtypeStruct((FIELDS, 2, 8, 256), F32),
        ),
        scratch_shapes=[
            pltpu.VMEM((VALUES * SLOTS, PEERS), F32),
            pltpu.VMEM((4, SLOTS, PEERS), F32),
            pltpu.VMEM((SLOTS, PEERS), F32),
            pltpu.VMEM((SLOTS, PEERS), F32),
            pltpu.VMEM((SLOTS, PEERS), F32),
            pltpu.VMEM((8, 256, 256), F32),
        ],
        compiler_params=params(24),
        name="deposit",
    )(arrived)


def y_pass(lattice, from_right, from_left, y_offset, y_frac):
    return pl.pallas_call(
        y_kernel,
        out_shape=jax.ShapeDtypeStruct(lattice.shape, F32),
        compiler_params=params(16),
        name="y_pass",
    )(lattice, from_right, from_left, y_offset, y_frac)


def per_device(fields, frac_x, owner, slab, line_in, xcell, tile_count, y_offset, y_frac):
    lines = lax.axis_size("lines")
    outgoing = bucket(fields, frac_x, owner, slab, line_in, xcell, tile_count)
    arrived = lax.all_to_all(outgoing, ("lines", "slab"), split_axis=0, concat_axis=0, tiled=True)
    lattice, low_edge, high_edge = deposit(arrived)
    from_left = lax.ppermute(high_edge, "lines", [(i, (i + 1) % lines) for i in range(lines)])
    from_right = lax.ppermute(low_edge, "lines", [(i, (i - 1) % lines) for i in range(lines)])
    return y_pass(lattice, from_right, from_left, y_offset, y_frac)


def solution(mesh):
    return jax.shard_map(
        per_device,
        mesh=mesh,
        in_specs=(
            P(None, ("lines", "slab")),
            P(("lines", "slab")),
            P(("lines", "slab")),
            P(("lines", "slab")),
            P(("lines", "slab")),
            P(("lines", "slab")),
            P(("lines", "slab")),
            P("lines", "slab", None),
            P("lines", "slab", None),
        ),
        out_specs=P(None, "lines", "slab", None),
        check_vma=False,
    )
```

```python
import functools

import jax
import jax.numpy as jnp
from jax import lax
from jax.experimental import pallas as pl
from jax.experimental.pallas import tpu as pltpu
from jax.sharding import PartitionSpec as P

F32 = jnp.float32
BF16 = jnp.bfloat16
NT = (((1,), (1,)), ((), ()))

FIELDS = 6
SLOTS = 48
VALUES = 8
PEERS = 256
CHUNK = 256
PLANES = 8
OWN = 8


def kernel_weights(offset):
    remain = 1.0 - offset
    return (
        -0.5 * offset * remain * remain,
        1.0 - 2.5 * offset * offset + 1.5 * offset * offset * offset,
        1.0 - 2.5 * remain * remain + 1.5 * remain * remain * remain,
        -0.5 * offset * offset * remain,
    )


def split(value):
    high = value.astype(BF16).astype(F32)
    return high, (value - high).astype(BF16).astype(F32)


def bucket_kernel(
    fields_h, frac_h, owner_h, slab_h, line_in_h, xcell_h, count_h, out,
    fields, frac, owner, slab, line_in, xcell, count, sems, key_s, rank_s, place_s, upper_s, acc,
):
    moves = [
        pltpu.make_async_copy(source, goal, sems.at[number])
        for number, (source, goal) in enumerate((
            (count_h, count), (slab_h, slab), (xcell_h, xcell), (owner_h, owner), (line_in_h, line_in), (frac_h, frac), (fields_h, fields),
        ))
    ]
    for move in moves:
        move.start()
    for move in moves:
        move.wait()
    rows = key_s.shape[0]
    lane = lax.broadcasted_iota(jnp.int32, key_s.shape, 1)
    tile = lax.broadcasted_iota(jnp.int32, (rows, rows), 0) == lax.broadcasted_iota(jnp.int32, (rows, rows), 1)
    alive = lane < jnp.sum(jnp.where(tile, count[...], 0), axis=1, keepdims=True)
    key = (xcell[...] >> 4) * 8 + slab[...]
    key_s[...] = jnp.where(alive, key, -1).astype(F32)
    place_s[0] = (owner[...] * 8 + (line_in[...] >> 3)).astype(F32)
    place_s[1] = ((128 + (line_in[...] & 7) * 16 + (xcell[...] & 15)) * 256).astype(F32)
    place_s[2], place_s[3] = split(frac[...])
    before = lax.broadcasted_iota(jnp.int32, (CHUNK, CHUNK), 0) < lax.broadcasted_iota(jnp.int32, (CHUNK, CHUNK), 1)
    upper_s[...] = jnp.where(before, 1.0, 0.0).astype(BF16)
    peer = lax.broadcasted_iota(jnp.int32, (PEERS, 128), 0).astype(F32)

    def row_of(ref, row):
        return ref[pl.ds(row, 1), :]

    def hits(row):
        return row_of(key_s, row) == peer

    unroll = 4

    def rank_step(step, base):
        for part in range(unroll):
            row = (step * unroll + part) * 2
            hit = [hits(row + half) for half in range(2)]
            one = jnp.concatenate([jnp.where(h, 1.0, 0.0).astype(BF16) for h in hit], axis=1)
            earlier = jnp.dot(one, upper_s[...], preferred_element_type=F32)
            for half in range(2):
                seen = earlier[:, half * 128:(half + 1) * 128] + base
                rank_s[pl.ds(row + half, 1), :] = jnp.sum(jnp.where(hit[half], seen, 0.0), axis=0, keepdims=True)
            base = base + jnp.dot(one, jnp.ones((CHUNK, 128), BF16), preferred_element_type=F32)
        return base

    lax.fori_loop(0, rows // (2 * unroll), rank_step, jnp.zeros((PEERS, 128), F32))

    slot = lax.broadcasted_iota(jnp.int32, (SLOTS, 128), 0).astype(F32)
    wide = 8
    acc[...] = jnp.zeros_like(acc)

    def send_step(step, carry):
        ones, packed = [], []
        for part in range(wide):
            row = step * wide + part
            ones.append(jnp.where(hits(row), 1.0, 0.0).astype(BF16))
            here = row_of(rank_s, row) == slot
            block = fields[:, pl.ds(pl.multiple_of(row * 128, 128), 128)]
            high, low = split(block)
            highs = [high[f:f + 1] for f in range(FIELDS)]
            lows = [low[f:f + 1] for f in range(FIELDS)]
            highs += [place_s[2, pl.ds(row, 1), :], place_s[0, pl.ds(row, 1), :]]
            lows += [place_s[3, pl.ds(row, 1), :], place_s[1, pl.ds(row, 1), :]]
            packed.append(jnp.concatenate([jnp.where(here, v, 0.0).astype(BF16) for v in highs + lows], axis=0))
        acc[...] += lax.dot_general(
            jnp.concatenate(packed, axis=1), jnp.concatenate(ones, axis=1), NT, preferred_element_type=F32
        )
        return carry

    lax.fori_loop(0, rows // wide, send_step, 0)
    half = VALUES * SLOTS
    total = acc[:half, :] + acc[half:, :]
    out[...] = jnp.swapaxes(total, 0, 1)[:, None, :]


def deposit_kernel(arrived, lattice, low_edge, high_edge, flat_s, plane_s, to_s, over_s, mine_s, weight_s, acc):
    flat_s[...] = jnp.swapaxes(arrived[:, 0, :], 0, 1)
    place = flat_s[7 * SLOTS:8 * SLOTS, :].astype(jnp.int32)
    live = place >= 32768
    plane = jnp.where(live, (place >> 12) & 7, 99).astype(F32)
    plane_s[...] = plane
    sub = lax.broadcasted_iota(jnp.int32, (8, PEERS), 0)
    subf = sub.astype(F32)
    seen = jnp.zeros((PLANES, PEERS), F32)
    for slot in range(SLOTS):
        hit = plane_s[slot:slot + 1, :] == subf
        to_s[slot:slot + 1, :] = jnp.sum(jnp.where(hit, seen, 0.0), axis=0, keepdims=True)
        seen = seen + jnp.where(hit, 1.0, 0.0)
    rank = to_s[...]
    fits = rank < OWN
    to_s[...] = jnp.where(fits, plane * OWN + rank, 9999.0)
    extra = jnp.logical_and(live, jnp.logical_not(fits))
    before = lax.broadcasted_iota(jnp.int32, (SLOTS, SLOTS), 1) < lax.broadcasted_iota(jnp.int32, (SLOTS, SLOTS), 0)
    order = jnp.dot(jnp.where(before, 1.0, 0.0).astype(BF16), jnp.where(extra, 1.0, 0.0).astype(BF16), preferred_element_type=F32)
    over_s[...] = jnp.where(extra, order, -1.0)
    rounds = jnp.max(jnp.where(extra, order, -1.0)).astype(jnp.int32) + 1

    low_rows = (sub + 1).astype(F32)
    high_rows = (sub + 9).astype(F32)
    edge_rows = jnp.where(sub % 4 == 0, 0, jnp.where(sub % 4 == 3, 99, 16 + sub % 4)).astype(F32)
    first = sub < 4
    y_iota = lax.broadcasted_iota(jnp.int32, (256, PEERS), 0).astype(F32)

    def rows_of(weights, xin, field):
        spread = []
        for nodes in (low_rows, high_rows, edge_rows):
            apart = nodes - xin
            value = jnp.zeros((8, PEERS), F32)
            for k in range(4):
                value = jnp.where(apart == float(k), weights[k], value)
            spread.append(value)
        groups = []
        for f in range(FIELDS):
            groups += [spread[0] * field[f], spread[1] * field[f]]
        for f in range(0, FIELDS, 2):
            groups.append(spread[2] * jnp.where(first, field[f], field[f + 1]))
        groups.append(jnp.zeros((8, PEERS), F32))
        whole = jnp.concatenate(groups, axis=0)
        high = whole.astype(BF16)
        low = (whole - high.astype(F32)).astype(BF16)
        return jnp.concatenate([high, low], axis=0)

    def planes_step(step, carry):
        pair = 2
        found = [[jnp.zeros((8, PEERS), F32) for _ in range(VALUES)] for _ in range(pair)]
        goal = [subf + ((step * pair + part) * OWN).astype(F32) for part in range(pair)]
        for slot in range(SLOTS):
            to = to_s[slot:slot + 1, :]
            rows = [flat_s[v * SLOTS + slot:v * SLOTS + slot + 1, :] for v in range(VALUES)]
            for part in range(pair):
                hit = to == goal[part]
                found[part] = [jnp.where(hit, rows[v], found[part][v]) for v in range(VALUES)]
        for part in range(pair):
            spot = found[part][7].astype(jnp.int32)
            for v in range(FIELDS):
                mine_s[part, v] = found[part][v]
            mine_s[part, 6] = ((spot >> 8) & 15).astype(F32)
            mine_s[part, 7] = (spot & 255).astype(F32)
            for number, weight in enumerate(kernel_weights(found[part][6])):
                weight_s[part, number] = weight
        for part in range(pair):
            packed, ones = [], []
            for own in range(OWN):
                row = lambda v: mine_s[part, v, own:own + 1, :]
                packed.append(rows_of([weight_s[part, k, own:own + 1, :] for k in range(4)], row(6), [row(f) for f in range(FIELDS)]))
                ones.append(jnp.where(row(7) == y_iota, 1.0, 0.0).astype(BF16))
            acc[step * pair + part] = lax.dot_general(
                jnp.concatenate(ones, axis=1), jnp.concatenate(packed, axis=1), NT, preferred_element_type=F32
            )
        return carry

    lax.fori_loop(0, PLANES // 2, planes_step, 0)

    def extra_step(number, carry):
        hit = over_s[...] == number.astype(F32)
        pick = lambda v: jnp.sum(jnp.where(hit, flat_s[v * SLOTS:(v + 1) * SLOTS, :], 0.0), axis=0, keepdims=True)
        field = [pick(f) for f in range(FIELDS)]
        weights = kernel_weights(pick(6))
        spot = pick(7).astype(jnp.int32)
        packed = rows_of(weights, ((spot >> 8) & 15).astype(F32), field)
        plane = (spot >> 12) & 7
        spot_y = (spot & 255).astype(F32)
        for z in range(PLANES):
            one = jnp.where(jnp.where(plane == z, spot_y, -1.0) == y_iota, 1.0, 0.0).astype(BF16)
            acc[z] += lax.dot_general(one, packed, NT, preferred_element_type=F32)
        return carry

    lax.fori_loop(0, rounds, extra_step, 0)
    for z in range(PLANES):
        nodes = jnp.swapaxes(acc[z, :, :128] + acc[z, :, 128:], 0, 1)
        for f in range(FIELDS):
            for half in range(2):
                at = (f * 2 + half) * 8
                lattice[f, half * 8:half * 8 + 8, z, :] = nodes[at:at + 8, :]
            at = 96 + f * 4
            low_edge[f, 0, z:z + 1, :] = nodes[at:at + 1, :]
            high_edge[f, 0, z:z + 1, :] = nodes[at + 1:at + 2, :]
            high_edge[f, 1, z:z + 1, :] = nodes[at + 2:at + 3, :]


def y_factors(y_offset, y_frac):
    weights = kernel_weights(y_frac)
    is_shift = [y_offset == s for s in range(-2, 3)]
    factors = []
    for travel in range(-3, 5):
        factor = jnp.zeros_like(weights[0])
        for s in range(-2, 3):
            if -1 <= travel - s <= 2:
                factor = jnp.where(is_shift[s + 2], weights[travel - s + 1], factor)
        factors.append(factor)
    return factors


def y_spread(values, factors):
    total = values * factors[3]
    for travel in range(-3, 5):
        if travel:
            total = total + pltpu.roll(values * factors[travel + 3], travel % values.shape[1], 1)
    return total


def y_inner_kernel(lattice, y_offset, y_frac, out, ready, sems):
    width = y_offset.shape[0]

    def body(x, carry):
        factors = y_factors(y_offset[x], y_frac[x])
        for f in range(FIELDS):
            ready[x, f] = y_spread(lattice[f, x], factors)
        pltpu.make_async_copy(ready.at[x], out.at[:, x], sems.at[x]).start()
        return carry

    lax.fori_loop(2, width - 1, body, 0)

    def drain(x, carry):
        pltpu.make_async_copy(ready.at[x], out.at[:, x], sems.at[x]).wait()
        return carry

    lax.fori_loop(2, width - 1, drain, 0)


def y_edge_kernel(lattice, from_right, from_left, y_offset, y_frac, partial, out, ready, sems):
    width = y_offset.shape[0]
    moves = []
    for number, (x, halo, at) in enumerate(((0, from_left, 0), (1, from_left, 1), (width - 1, from_right, 0))):
        factors = y_factors(y_offset[x], y_frac[x])
        for f in range(FIELDS):
            ready[f, number] = y_spread(lattice[f, x] + halo[f, at], factors)
        moves.append(pltpu.make_async_copy(ready.at[:, number], out.at[:, x], sems.at[number]))
        moves[-1].start()
    for move in moves:
        move.wait()


def params(mib):
    return pltpu.CompilerParams(vmem_limit_bytes=mib << 20)


def bucket(fields, frac, owner, slab, line_in, xcell, count):
    rows = frac.shape[0] // 128
    grid2 = lambda v: v.reshape(rows, 128)
    return pl.pallas_call(
        bucket_kernel,
        out_shape=jax.ShapeDtypeStruct((PEERS, 1, VALUES * SLOTS), F32),
        in_specs=[pl.BlockSpec(memory_space=pltpu.HBM)] * 7,
        scratch_shapes=[
            pltpu.VMEM(fields.shape, F32),
            pltpu.VMEM((rows, 128), F32),
            pltpu.VMEM((rows, 128), jnp.int32),
            pltpu.VMEM((rows, 128), jnp.int32),
            pltpu.VMEM((rows, 128), jnp.int32),
            pltpu.VMEM((rows, 128), jnp.int32),
            pltpu.VMEM((1, rows), jnp.int32),
            pltpu.SemaphoreType.DMA((7,)),
            pltpu.VMEM((rows, 128), F32),
            pltpu.VMEM((rows, 128), F32),
            pltpu.VMEM((4, rows, 128), F32),
            pltpu.VMEM((CHUNK, CHUNK), BF16),
            pltpu.VMEM((2 * VALUES * SLOTS, PEERS), F32),
        ],
        compiler_params=params(56),
        name="bucket",
    )(fields, grid2(frac), grid2(owner), grid2(slab), grid2(line_in), grid2(xcell), count.reshape(1, rows))


def deposit(arrived):
    return pl.pallas_call(
        deposit_kernel,
        out_shape=(
            jax.ShapeDtypeStruct((FIELDS, 16, 8, 256), F32),
            jax.ShapeDtypeStruct((FIELDS, 1, 8, 256), F32),
            jax.ShapeDtypeStruct((FIELDS, 2, 8, 256), F32),
        ),
        scratch_shapes=[
            pltpu.VMEM((VALUES * SLOTS, PEERS), F32),
            pltpu.VMEM((SLOTS, PEERS), F32),
            pltpu.VMEM((SLOTS, PEERS), F32),
            pltpu.VMEM((SLOTS, PEERS), F32),
            pltpu.VMEM((2, VALUES, 8, PEERS), F32),
            pltpu.VMEM((2, 4, 8, PEERS), F32),
            pltpu.VMEM((8, 256, 256), F32),
        ],
        compiler_params=params(24),
        name="deposit",
    )(arrived)


def y_inner(lattice, y_offset, y_frac):
    return pl.pallas_call(
        y_inner_kernel,
        out_shape=jax.ShapeDtypeStruct(lattice.shape, F32),
        out_specs=pl.BlockSpec(memory_space=pltpu.HBM),
        scratch_shapes=[
            pltpu.VMEM((lattice.shape[1], FIELDS) + lattice.shape[2:], F32),
            pltpu.SemaphoreType.DMA((lattice.shape[1],)),
        ],
        compiler_params=params(16),
        cost_estimate=pl.CostEstimate(flops=20 * lattice.size, bytes_accessed=8 * lattice.size, transcendentals=0),
        name="y_inner",
    )(lattice, y_offset, y_frac)


def y_edge(lattice, from_right, from_left, y_offset, y_frac, partial):
    vmem = pl.BlockSpec(memory_space=pltpu.VMEM)
    return pl.pallas_call(
        y_edge_kernel,
        out_shape=jax.ShapeDtypeStruct(lattice.shape, F32),
        in_specs=[vmem] * 5 + [pl.BlockSpec(memory_space=pltpu.HBM)],
        out_specs=pl.BlockSpec(memory_space=pltpu.HBM),
        input_output_aliases={5: 0},
        scratch_shapes=[
            pltpu.VMEM((FIELDS, 3) + lattice.shape[2:], F32),
            pltpu.SemaphoreType.DMA((3,)),
        ],
        compiler_params=params(16),
        name="y_edge",
    )(lattice, from_right, from_left, y_offset, y_frac, partial)


def per_device(fields, frac_x, owner, slab, line_in, xcell, tile_count, y_offset, y_frac):
    lines = lax.axis_size("lines")
    outgoing = bucket(fields, frac_x, owner, slab, line_in, xcell, tile_count)
    arrived = lax.all_to_all(outgoing, ("lines", "slab"), split_axis=0, concat_axis=0, tiled=True)
    lattice, low_edge, high_edge = deposit(arrived)
    from_left = lax.ppermute(high_edge, "lines", [(i, (i + 1) % lines) for i in range(lines)])
    from_right = lax.ppermute(low_edge, "lines", [(i, (i - 1) % lines) for i in range(lines)])
    partial = y_inner(lattice, y_offset, y_frac)
    return y_edge(lattice, from_right, from_left, y_offset, y_frac, partial)


def solution(mesh):
    return jax.shard_map(
        per_device,
        mesh=mesh,
        in_specs=(
            P(None, ("lines", "slab")),
            P(("lines", "slab")),
            P(("lines", "slab")),
            P(("lines", "slab")),
            P(("lines", "slab")),
            P(("lines", "slab")),
            P(("lines", "slab")),
            P("lines", "slab", None),
            P("lines", "slab", None),
        ),
        out_specs=P(None, "lines", "slab", None),
        check_vma=False,
    )
```

```python
import functools

import jax
import jax.numpy as jnp
from jax import lax
from jax.experimental import pallas as pl
from jax.experimental.pallas import tpu as pltpu
from jax.sharding import PartitionSpec as P

F32 = jnp.float32
BF16 = jnp.bfloat16
NT = (((1,), (1,)), ((), ()))

FIELDS = 6
SLOTS = 48
VALUES = 8
PEERS = 256
PLANES = 8
OWN = 7


def kernel_weights(offset):
    remain = 1.0 - offset
    return (
        -0.5 * offset * remain * remain,
        1.0 - 2.5 * offset * offset + 1.5 * offset * offset * offset,
        1.0 - 2.5 * remain * remain + 1.5 * remain * remain * remain,
        -0.5 * offset * offset * remain,
    )


def split(value):
    high = value.astype(BF16).astype(F32)
    return high, (value - high).astype(BF16).astype(F32)


def bucket_kernel(
    fields_h, frac_h, owner_h, slab_h, line_in_h, xcell_h, count_h, out,
    fields, frac, owner, slab, line_in, xcell, count, sems, key_s, rank_s, place_s, hot_s, hist_s, acc,
):
    moves = [
        pltpu.make_async_copy(source, goal, sems.at[number])
        for number, (source, goal) in enumerate((
            (count_h, count), (slab_h, slab), (xcell_h, xcell), (owner_h, owner), (line_in_h, line_in), (frac_h, frac),
            (fields_h, fields),
        ))
    ]
    for move in moves:
        move.start()
    for move in moves[:3]:
        move.wait()
    rows = key_s.shape[0]
    lane = lax.broadcasted_iota(jnp.int32, key_s.shape, 1)
    tile = lax.broadcasted_iota(jnp.int32, (rows, rows), 0) == lax.broadcasted_iota(jnp.int32, (rows, rows), 1)
    alive = lane < jnp.sum(jnp.where(tile, count[...], 0), axis=1, keepdims=True)
    key_s[...] = jnp.where(alive, (xcell[...] >> 4) * 8 + slab[...], -1).astype(F32)
    sixteen = lax.broadcasted_iota(jnp.int32, (16, 128), 0).astype(F32)
    one, zero = jnp.ones((), BF16), jnp.zeros((), BF16)

    def wide_row(row):
        return jnp.broadcast_to(row, (16, 128)).astype(BF16)

    hist_s[...] = jnp.zeros_like(hist_s)
    unroll = 4

    def hot_step(step, carry):
        total = hist_s[...]
        for part in range(unroll):
            row = step * unroll + part
            key = wide_row(key_s[pl.ds(row, 1), :])
            hot = jnp.concatenate(
                [jnp.where(key == (sixteen + 16.0 * g).astype(BF16), one, zero) for g in range(PEERS // 16)], axis=0
            )
            hot_s[:, pl.ds(pl.multiple_of(row * 128, 128), 128)] = hot
            total = total + hot
        hist_s[...] = total
        return carry

    lax.fori_loop(0, rows // unroll, hot_step, 0)
    earlier = lax.broadcasted_iota(jnp.int32, (128, 128), 0) < lax.broadcasted_iota(jnp.int32, (128, 128), 1)
    base = jnp.dot(hist_s[...], jnp.where(earlier, 1.0, 0.0).astype(BF16), preferred_element_type=F32)
    hist_s[...] = base.astype(BF16)
    sub = lax.broadcasted_iota(jnp.int32, (8, 128), 0)
    groups = rows // 8
    keys = [key_s[g * 8:g * 8 + 8, :] for g in range(groups)]
    above = [jnp.zeros((8, 128), F32) for _ in range(groups)]
    for row in range(rows):
        key = key_s[row:row + 1, :]
        for g in range(row // 8, groups):
            same = keys[g] == key
            if g == row // 8:
                same = jnp.logical_and(same, sub > row % 8)
            above[g] = above[g] + jnp.where(same, 1.0, 0.0)
    for g in range(groups):
        rank_s[g * 8:g * 8 + 8, :] = above[g]

    for move in moves[3:]:
        move.wait()
    place_s[0] = (owner[...] * 8 + (line_in[...] >> 3)).astype(F32)
    place_s[1] = ((128 + (line_in[...] & 7) * 16 + (xcell[...] & 15)) * 256).astype(F32)
    place_s[2], place_s[3] = split(frac[...])
    wide = 8
    acc[...] = jnp.zeros_like(acc)

    for step in range(rows // wide):
        packed = []
        for part in range(wide):
            row = step * wide + part
            columns = pl.ds(row * 128, 128)
            seen = hot_s[:, columns] * hist_s[...]
            some = seen[0:16]
            for g in range(1, PEERS // 16):
                some = some + seen[g * 16:g * 16 + 16]
            rank = jnp.sum(some.astype(F32), axis=0, keepdims=True) + rank_s[row:row + 1, :]
            rank = wide_row(rank)
            here = [rank == (sixteen + 16.0 * g).astype(BF16) for g in range(SLOTS // 16)]
            high, low = split(fields[:, columns])
            highs = [high[f:f + 1] for f in range(FIELDS)]
            lows = [low[f:f + 1] for f in range(FIELDS)]
            highs += [place_s[2, row:row + 1, :], place_s[0, row:row + 1, :]]
            lows += [place_s[3, row:row + 1, :], place_s[1, row:row + 1, :]]
            pieces = []
            for v in highs + lows:
                v = wide_row(v)
                pieces += [jnp.where(h, v, zero) for h in here]
            packed.append(jnp.concatenate(pieces, axis=0))
        block = hot_s[:, pl.ds(step * wide * 128, wide * 128)]
        acc[...] += lax.dot_general(jnp.concatenate(packed, axis=1), block, NT, preferred_element_type=F32)
    half = VALUES * SLOTS
    total = acc[:half, :] + acc[half:, :]
    out[...] = jnp.swapaxes(total, 0, 1)[:, None, :]


def deposit_kernel(arrived, lattice, low_edge, high_edge, flat_s, plane_s, to_s, over_s, mine_s, weight_s, acc):
    flat_s[...] = jnp.swapaxes(arrived[:, 0, :], 0, 1)
    place = flat_s[7 * SLOTS:8 * SLOTS, :].astype(jnp.int32)
    live = place >= 32768
    plane = jnp.where(live, (place >> 12) & 7, 99).astype(F32)
    plane_s[...] = plane
    sub = lax.broadcasted_iota(jnp.int32, (8, PEERS), 0)
    subf = sub.astype(F32)
    seen = jnp.zeros((PLANES, PEERS), F32)
    for slot in range(SLOTS):
        hit = plane_s[slot:slot + 1, :] == subf
        to_s[slot:slot + 1, :] = jnp.sum(jnp.where(hit, seen, 0.0), axis=0, keepdims=True)
        seen = seen + jnp.where(hit, 1.0, 0.0)
    rank = to_s[...]
    fits = rank < OWN
    to_s[...] = jnp.where(fits, plane * 8 + rank, 9999.0)
    extra = jnp.logical_and(live, jnp.logical_not(fits))
    before = lax.broadcasted_iota(jnp.int32, (SLOTS, SLOTS), 1) < lax.broadcasted_iota(jnp.int32, (SLOTS, SLOTS), 0)
    order = jnp.dot(jnp.where(before, 1.0, 0.0).astype(BF16), jnp.where(extra, 1.0, 0.0).astype(BF16), preferred_element_type=F32)
    over_s[...] = jnp.where(extra, order, -1.0)
    left = jnp.sum(jnp.maximum(seen - OWN, 0.0), axis=0, keepdims=True)
    most = jnp.max(left, axis=1, keepdims=True)
    few = jnp.logical_and(jnp.sum(left, axis=1, keepdims=True) <= PEERS, most <= 8)
    rounds = jnp.max(jnp.where(few, 0.0, most)).astype(jnp.int32)

    low_rows = (sub + 1).astype(F32)
    high_rows = (sub + 9).astype(F32)
    edge_rows = jnp.where(sub % 4 == 0, 0, jnp.where(sub % 4 == 3, 99, 16 + sub % 4)).astype(F32)
    first = sub < 4
    sixteen = lax.broadcasted_iota(jnp.int32, (16, PEERS), 0).astype(F32)
    levels = [(sixteen + 16.0 * g).astype(BF16) for g in range(16)]

    one, zero = jnp.ones((), BF16), jnp.zeros((), BF16)

    def hot(row):
        row = jnp.broadcast_to(row, (16, PEERS)).astype(BF16)
        return jnp.concatenate([jnp.where(row == level, one, zero) for level in levels], axis=0)

    def rows_of(weights, xin, field):
        spread = []
        for nodes in (low_rows, high_rows, edge_rows):
            apart = nodes - xin
            value = jnp.zeros((8, PEERS), F32)
            for k in range(4):
                value = jnp.where(apart == float(k), weights[k], value)
            spread.append(value)
        groups = []
        for f in range(FIELDS):
            groups += [spread[0] * field[f], spread[1] * field[f]]
        for f in range(0, FIELDS, 2):
            groups.append(spread[2] * jnp.where(first, field[f], field[f + 1]))
        groups.append(jnp.zeros((8, PEERS), F32))
        whole = jnp.concatenate(groups, axis=0)
        high = whole.astype(BF16)
        low = (whole - high.astype(F32)).astype(BF16)
        return jnp.concatenate([high, low], axis=0)

    def gather(goals):
        found = [[jnp.zeros((8, PEERS), F32) for _ in range(VALUES)] for _ in goals]
        for slot in range(SLOTS):
            rows = [flat_s[v * SLOTS + slot:v * SLOTS + slot + 1, :] for v in range(VALUES)]
            for part, (numbers, goal) in enumerate(goals):
                hit = numbers[slot:slot + 1, :] == goal
                found[part] = [jnp.where(hit, rows[v], found[part][v]) for v in range(VALUES)]
        return found

    found = gather([(over_s, subf)])[0]
    pieces = [split(v) for v in found]
    stack = jnp.concatenate([p[0] for p in pieces] + [p[1] for p in pieces], axis=0).astype(BF16)
    lanes = lax.broadcasted_iota(jnp.int32, (PEERS, PEERS), 0)
    ahead = jnp.where(lanes < lax.broadcasted_iota(jnp.int32, (PEERS, PEERS), 1), 1.0, 0.0).astype(BF16)
    start = jnp.dot(jnp.broadcast_to(left, (16, PEERS)).astype(BF16), ahead, preferred_element_type=F32)[0:1]
    picked = [jnp.zeros((8, PEERS), F32) for _ in range(VALUES)]
    for k in range(8):
        spot = jnp.where(jnp.logical_and(left > k, few), start + k, -1.0)
        moved = lax.dot_general(stack, hot(spot), NT, preferred_element_type=F32)
        for v in range(VALUES):
            value = moved[v * 8:v * 8 + 8] + moved[(VALUES + v) * 8:(VALUES + v) * 8 + 8]
            picked[v] = jnp.where(sub == k, value, picked[v])
    picked = [jnp.sum(v, axis=0, keepdims=True) for v in picked]
    spot = picked[7].astype(jnp.int32)
    few_rows = rows_of(kernel_weights(picked[6]), ((spot >> 8) & 15).astype(F32), picked[:FIELDS])
    few_plane = (spot >> 12) & 7
    few_y = (spot & 255).astype(F32)

    pair = 2
    for step in range(PLANES // pair):
        found = gather([(to_s, subf + float((step * pair + part) * 8)) for part in range(pair)])
        for part in range(pair):
            spot = found[part][7].astype(jnp.int32)
            z = step * pair + part
            for v in range(FIELDS):
                mine_s[z, v] = found[part][v]
            mine_s[z, 6] = ((spot >> 8) & 15).astype(F32)
            mine_s[z, 7] = (spot & 255).astype(F32)
            for number, weight in enumerate(kernel_weights(found[part][6])):
                weight_s[z, number] = weight
    for z in range(PLANES):
        packed, ones = [few_rows], [hot(jnp.where(few_plane == z, few_y, -1.0))]
        for own in range(OWN):
            row = lambda v: mine_s[z, v, own:own + 1, :]
            packed.append(rows_of([weight_s[z, k, own:own + 1, :] for k in range(4)], row(6), [row(f) for f in range(FIELDS)]))
            ones.append(hot(row(7)))
        acc[z] = lax.dot_general(
            jnp.concatenate(ones, axis=1), jnp.concatenate(packed, axis=1), NT, preferred_element_type=F32
        )

    def extra_step(number, carry):
        hit = over_s[...] == number.astype(F32)
        pick = lambda v: jnp.sum(jnp.where(hit, flat_s[v * SLOTS:(v + 1) * SLOTS, :], 0.0), axis=0, keepdims=True)
        field = [pick(f) for f in range(FIELDS)]
        weights = kernel_weights(pick(6))
        spot = pick(7).astype(jnp.int32)
        packed = rows_of(weights, ((spot >> 8) & 15).astype(F32), field)
        plane = (spot >> 12) & 7
        spot_y = (spot & 255).astype(F32)
        for z in range(PLANES):
            acc[z] += lax.dot_general(hot(jnp.where(plane == z, spot_y, -1.0)), packed, NT, preferred_element_type=F32)
        return carry

    lax.fori_loop(0, rounds, extra_step, 0)
    for z in range(PLANES):
        nodes = jnp.swapaxes(acc[z, :, :128] + acc[z, :, 128:], 0, 1)
        for f in range(FIELDS):
            for half in range(2):
                at = (f * 2 + half) * 8
                lattice[f, half * 8:half * 8 + 8, z, :] = nodes[at:at + 8, :]
            at = 96 + f * 4
            low_edge[f, 0, z:z + 1, :] = nodes[at:at + 1, :]
            high_edge[f, 0, z:z + 1, :] = nodes[at + 1:at + 2, :]
            high_edge[f, 1, z:z + 1, :] = nodes[at + 2:at + 3, :]


def y_factors(y_offset, y_frac):
    weights = kernel_weights(y_frac)
    is_shift = [y_offset == s for s in range(-2, 3)]
    factors = []
    for travel in range(-3, 5):
        factor = jnp.zeros_like(weights[0])
        for s in range(-2, 3):
            if -1 <= travel - s <= 2:
                factor = jnp.where(is_shift[s + 2], weights[travel - s + 1], factor)
        factors.append(factor)
    return factors


def y_spread(values, factors):
    total = values * factors[3]
    for travel in range(-3, 5):
        if travel:
            total = total + pltpu.roll(values * factors[travel + 3], travel % values.shape[1], 1)
    return total


def y_inner_kernel(lattice, y_offset, y_frac, out, ready, sems):
    width = y_offset.shape[0]

    def body(x, carry):
        factors = y_factors(y_offset[x], y_frac[x])
        for f in range(FIELDS):
            ready[x, f] = y_spread(lattice[f, x], factors)
        pltpu.make_async_copy(ready.at[x], out.at[:, x], sems.at[x]).start()
        return carry

    lax.fori_loop(2, width - 1, body, 0)

    def drain(x, carry):
        pltpu.make_async_copy(ready.at[x], out.at[:, x], sems.at[x]).wait()
        return carry

    lax.fori_loop(2, width - 1, drain, 0)


def y_edge_kernel(lattice, from_right, from_left, y_offset, y_frac, partial, out, ready, sems):
    width = y_offset.shape[0]
    moves = []
    for number, (x, halo, at) in enumerate(((0, from_left, 0), (1, from_left, 1), (width - 1, from_right, 0))):
        factors = y_factors(y_offset[x], y_frac[x])
        for f in range(FIELDS):
            ready[f, number] = y_spread(lattice[f, x] + halo[f, at], factors)
        moves.append(pltpu.make_async_copy(ready.at[:, number], out.at[:, x], sems.at[number]))
        moves[-1].start()
    for move in moves:
        move.wait()


def params(mib):
    return pltpu.CompilerParams(vmem_limit_bytes=mib << 20)


def bucket(fields, frac, owner, slab, line_in, xcell, count):
    rows = frac.shape[0] // 128
    grid2 = lambda v: v.reshape(rows, 128)
    return pl.pallas_call(
        bucket_kernel,
        out_shape=jax.ShapeDtypeStruct((PEERS, 1, VALUES * SLOTS), F32),
        in_specs=[pl.BlockSpec(memory_space=pltpu.HBM)] * 7,
        scratch_shapes=[
            pltpu.VMEM(fields.shape, F32),
            pltpu.VMEM((rows, 128), F32),
            pltpu.VMEM((rows, 128), jnp.int32),
            pltpu.VMEM((rows, 128), jnp.int32),
            pltpu.VMEM((rows, 128), jnp.int32),
            pltpu.VMEM((rows, 128), jnp.int32),
            pltpu.VMEM((1, rows), jnp.int32),
            pltpu.SemaphoreType.DMA((7,)),
            pltpu.VMEM((rows, 128), F32),
            pltpu.VMEM((rows, 128), F32),
            pltpu.VMEM((4, rows, 128), F32),
            pltpu.VMEM((PEERS, rows * 128), BF16),
            pltpu.VMEM((PEERS, 128), BF16),
            pltpu.VMEM((2 * VALUES * SLOTS, PEERS), F32),
        ],
        compiler_params=params(56),
        name="bucket",
    )(fields, grid2(frac), grid2(owner), grid2(slab), grid2(line_in), grid2(xcell), count.reshape(1, rows))


def deposit(arrived):
    return pl.pallas_call(
        deposit_kernel,
        out_shape=(
            jax.ShapeDtypeStruct((FIELDS, 16, 8, 256), F32),
            jax.ShapeDtypeStruct((FIELDS, 1, 8, 256), F32),
            jax.ShapeDtypeStruct((FIELDS, 2, 8, 256), F32),
        ),
        scratch_shapes=[
            pltpu.VMEM((VALUES * SLOTS, PEERS), F32),
            pltpu.VMEM((SLOTS, PEERS), F32),
            pltpu.VMEM((SLOTS, PEERS), F32),
            pltpu.VMEM((SLOTS, PEERS), F32),
            pltpu.VMEM((PLANES, VALUES, 8, PEERS), F32),
            pltpu.VMEM((PLANES, 4, 8, PEERS), F32),
            pltpu.VMEM((8, 256, 256), F32),
        ],
        compiler_params=params(24),
        name="deposit",
    )(arrived)


def y_inner(lattice, y_offset, y_frac):
    return pl.pallas_call(
        y_inner_kernel,
        out_shape=jax.ShapeDtypeStruct(lattice.shape, F32),
        out_specs=pl.BlockSpec(memory_space=pltpu.HBM),
        scratch_shapes=[
            pltpu.VMEM((lattice.shape[1], FIELDS) + lattice.shape[2:], F32),
            pltpu.SemaphoreType.DMA((lattice.shape[1],)),
        ],
        compiler_params=params(16),
        cost_estimate=pl.CostEstimate(flops=20 * lattice.size, bytes_accessed=8 * lattice.size, transcendentals=0),
        name="y_inner",
    )(lattice, y_offset, y_frac)


def y_edge(lattice, from_right, from_left, y_offset, y_frac, partial):
    vmem = pl.BlockSpec(memory_space=pltpu.VMEM)
    return pl.pallas_call(
        y_edge_kernel,
        out_shape=jax.ShapeDtypeStruct(lattice.shape, F32),
        in_specs=[vmem] * 5 + [pl.BlockSpec(memory_space=pltpu.HBM)],
        out_specs=pl.BlockSpec(memory_space=pltpu.HBM),
        input_output_aliases={5: 0},
        scratch_shapes=[
            pltpu.VMEM((FIELDS, 3) + lattice.shape[2:], F32),
            pltpu.SemaphoreType.DMA((3,)),
        ],
        compiler_params=params(16),
        name="y_edge",
    )(lattice, from_right, from_left, y_offset, y_frac, partial)


def per_device(fields, frac_x, owner, slab, line_in, xcell, tile_count, y_offset, y_frac):
    lines = lax.axis_size("lines")
    outgoing = bucket(fields, frac_x, owner, slab, line_in, xcell, tile_count)
    arrived = lax.all_to_all(outgoing, ("lines", "slab"), split_axis=0, concat_axis=0, tiled=True)
    lattice, low_edge, high_edge = deposit(arrived)
    from_left = lax.ppermute(high_edge, "lines", [(i, (i + 1) % lines) for i in range(lines)])
    from_right = lax.ppermute(low_edge, "lines", [(i, (i - 1) % lines) for i in range(lines)])
    partial = y_inner(lattice, y_offset, y_frac)
    return y_edge(lattice, from_right, from_left, y_offset, y_frac, partial)


def solution(mesh):
    return jax.shard_map(
        per_device,
        mesh=mesh,
        in_specs=(
            P(None, ("lines", "slab")),
            P(("lines", "slab")),
            P(("lines", "slab")),
            P(("lines", "slab")),
            P(("lines", "slab")),
            P(("lines", "slab")),
            P(("lines", "slab")),
            P("lines", "slab", None),
            P("lines", "slab", None),
        ),
        out_specs=P(None, "lines", "slab", None),
        check_vma=False,
    )
```

```python
import functools

import jax
import jax.numpy as jnp
from jax import lax
from jax.experimental import pallas as pl
from jax.experimental.pallas import tpu as pltpu
from jax.sharding import PartitionSpec as P

F32 = jnp.float32
BF16 = jnp.bfloat16
NT = (((1,), (1,)), ((), ()))

FIELDS = 6
SLOTS = 48
VALUES = 8
PEERS = 256
PLANES = 8
OWN = 6


def kernel_weights(offset):
    remain = 1.0 - offset
    return (
        -0.5 * offset * remain * remain,
        1.0 - 2.5 * offset * offset + 1.5 * offset * offset * offset,
        1.0 - 2.5 * remain * remain + 1.5 * remain * remain * remain,
        -0.5 * offset * offset * remain,
    )


def split(value):
    high = value.astype(BF16).astype(F32)
    return high, (value - high).astype(BF16).astype(F32)


def bucket_kernel(
    fields_h, frac_h, owner_h, slab_h, line_in_h, xcell_h, count_h, out,
    fields, frac, owner, slab, line_in, xcell, count, sems, key_s, rank_s, place_s, hot_s, hist_s, acc,
):
    moves = [
        pltpu.make_async_copy(source, goal, sems.at[number])
        for number, (source, goal) in enumerate((
            (count_h, count), (slab_h, slab), (xcell_h, xcell), (owner_h, owner), (line_in_h, line_in), (frac_h, frac),
            (fields_h, fields),
        ))
    ]
    for move in moves:
        move.start()
    for move in moves[:3]:
        move.wait()
    rows = key_s.shape[0]
    lane = lax.broadcasted_iota(jnp.int32, key_s.shape, 1)
    tile = lax.broadcasted_iota(jnp.int32, (rows, rows), 0) == lax.broadcasted_iota(jnp.int32, (rows, rows), 1)
    alive = lane < jnp.sum(jnp.where(tile, count[...], 0), axis=1, keepdims=True)
    key_s[...] = jnp.where(alive, (xcell[...] >> 4) * 8 + slab[...], -1).astype(F32)
    sixteen = lax.broadcasted_iota(jnp.int32, (16, 128), 0).astype(F32)
    one, zero = jnp.ones((), BF16), jnp.zeros((), BF16)

    def wide_row(row):
        return jnp.broadcast_to(row, (16, 128)).astype(BF16)

    hist_s[...] = jnp.zeros_like(hist_s)
    unroll = 4

    def hot_step(step, carry):
        total = hist_s[...]
        for part in range(unroll):
            row = step * unroll + part
            key = wide_row(key_s[pl.ds(row, 1), :])
            hot = jnp.concatenate(
                [jnp.where(key == (sixteen + 16.0 * g).astype(BF16), one, zero) for g in range(PEERS // 16)], axis=0
            )
            hot_s[:, pl.ds(pl.multiple_of(row * 128, 128), 128)] = hot
            total = total + hot
        hist_s[...] = total
        return carry

    lax.fori_loop(0, rows // unroll, hot_step, 0)
    earlier = lax.broadcasted_iota(jnp.int32, (128, 128), 0) < lax.broadcasted_iota(jnp.int32, (128, 128), 1)
    base = jnp.dot(hist_s[...], jnp.where(earlier, 1.0, 0.0).astype(BF16), preferred_element_type=F32)
    hist_s[...] = base.astype(BF16)
    sub = lax.broadcasted_iota(jnp.int32, (8, 128), 0)
    groups = rows // 8
    keys = [key_s[g * 8:g * 8 + 8, :] for g in range(groups)]
    above = [jnp.zeros((8, 128), F32) for _ in range(groups)]
    for row in range(rows):
        key = key_s[row:row + 1, :]
        for g in range(row // 8, groups):
            same = keys[g] == key
            if g == row // 8:
                same = jnp.logical_and(same, sub > row % 8)
            above[g] = above[g] + jnp.where(same, 1.0, 0.0)
    for g in range(groups):
        rank_s[g * 8:g * 8 + 8, :] = above[g]

    for move in moves[3:]:
        move.wait()
    place_s[0] = (owner[...] * 8 + (line_in[...] >> 3)).astype(F32)
    place_s[1] = ((128 + (line_in[...] & 7) * 16 + (xcell[...] & 15)) * 256).astype(F32)
    place_s[2], place_s[3] = split(frac[...])
    wide = 8
    acc[...] = jnp.zeros_like(acc)

    for step in range(rows // wide):
        packed = []
        for part in range(wide):
            row = step * wide + part
            columns = pl.ds(row * 128, 128)
            seen = hot_s[:, columns] * hist_s[...]
            some = seen[0:16]
            for g in range(1, PEERS // 16):
                some = some + seen[g * 16:g * 16 + 16]
            rank = jnp.sum(some.astype(F32), axis=0, keepdims=True) + rank_s[row:row + 1, :]
            rank = wide_row(rank)
            here = [rank == (sixteen + 16.0 * g).astype(BF16) for g in range(SLOTS // 16)]
            high, low = split(fields[:, columns])
            highs = [high[f:f + 1] for f in range(FIELDS)]
            lows = [low[f:f + 1] for f in range(FIELDS)]
            highs += [place_s[2, row:row + 1, :], place_s[0, row:row + 1, :]]
            lows += [place_s[3, row:row + 1, :], place_s[1, row:row + 1, :]]
            pieces = []
            for v in highs + lows:
                v = wide_row(v)
                pieces += [jnp.where(h, v, zero) for h in here]
            packed.append(jnp.concatenate(pieces, axis=0))
        block = hot_s[:, pl.ds(step * wide * 128, wide * 128)]
        acc[...] += lax.dot_general(jnp.concatenate(packed, axis=1), block, NT, preferred_element_type=F32)
    half = VALUES * SLOTS
    total = acc[:half, :] + acc[half:, :]
    out[...] = jnp.swapaxes(total, 0, 1)[:, None, :]


def deposit_kernel(arrived, lattice, low_edge, high_edge, flat_s, plane_s, to_s, over_s, mine_s, weight_s, acc):
    flat_s[...] = jnp.swapaxes(arrived[:, 0, :], 0, 1)
    place = flat_s[7 * SLOTS:8 * SLOTS, :].astype(jnp.int32)
    live = place >= 32768
    plane = jnp.where(live, (place >> 12) & 7, 99).astype(F32)
    plane_s[...] = plane
    sub = lax.broadcasted_iota(jnp.int32, (8, PEERS), 0)
    subf = sub.astype(F32)
    seen = jnp.zeros((PLANES, PEERS), F32)
    for slot in range(SLOTS):
        hit = plane_s[slot:slot + 1, :] == subf
        to_s[slot:slot + 1, :] = jnp.sum(jnp.where(hit, seen, 0.0), axis=0, keepdims=True)
        seen = seen + jnp.where(hit, 1.0, 0.0)
    rank = to_s[...]
    fits = rank < OWN
    to_s[...] = jnp.where(fits, plane * 8 + rank, 9999.0)
    extra = jnp.logical_and(live, jnp.logical_not(fits))
    before = lax.broadcasted_iota(jnp.int32, (SLOTS, SLOTS), 1) < lax.broadcasted_iota(jnp.int32, (SLOTS, SLOTS), 0)
    order = jnp.dot(jnp.where(before, 1.0, 0.0).astype(BF16), jnp.where(extra, 1.0, 0.0).astype(BF16), preferred_element_type=F32)
    over_s[...] = jnp.where(extra, order, -1.0)
    left = jnp.sum(jnp.maximum(seen - OWN, 0.0), axis=0, keepdims=True)
    most = jnp.max(left, axis=1, keepdims=True)
    few = jnp.logical_and(jnp.sum(left, axis=1, keepdims=True) <= PEERS, most <= 16)
    rounds = jnp.max(jnp.where(few, 0.0, most)).astype(jnp.int32)

    low_rows = (sub + 1).astype(F32)
    high_rows = (sub + 9).astype(F32)
    edge_rows = jnp.where(sub % 4 == 0, 0, jnp.where(sub % 4 == 3, 99, 16 + sub % 4)).astype(F32)
    first = sub < 4
    sixteen = lax.broadcasted_iota(jnp.int32, (16, PEERS), 0).astype(F32)
    levels = [(sixteen + 16.0 * g).astype(BF16) for g in range(16)]

    one, zero = jnp.ones((), BF16), jnp.zeros((), BF16)

    def hot(row):
        row = jnp.broadcast_to(row, (16, PEERS)).astype(BF16)
        return jnp.concatenate([jnp.where(row == level, one, zero) for level in levels], axis=0)

    def rows_of(weights, xin, field):
        spread = []
        for nodes in (low_rows, high_rows, edge_rows):
            apart = nodes - xin
            value = jnp.zeros((8, PEERS), F32)
            for k in range(4):
                value = jnp.where(apart == float(k), weights[k], value)
            spread.append(value)
        groups = []
        for f in range(FIELDS):
            groups += [spread[0] * field[f], spread[1] * field[f]]
        for f in range(0, FIELDS, 2):
            groups.append(spread[2] * jnp.where(first, field[f], field[f + 1]))
        groups.append(jnp.zeros((8, PEERS), F32))
        whole = jnp.concatenate(groups, axis=0)
        high = whole.astype(BF16)
        low = (whole - high.astype(F32)).astype(BF16)
        return jnp.concatenate([high, low], axis=0)

    def gather(goals):
        found = [[jnp.zeros((8, PEERS), F32) for _ in range(VALUES)] for _ in goals]
        for slot in range(SLOTS):
            rows = [flat_s[v * SLOTS + slot:v * SLOTS + slot + 1, :] for v in range(VALUES)]
            for part, (numbers, goal) in enumerate(goals):
                hit = numbers[slot:slot + 1, :] == goal
                found[part] = [jnp.where(hit, rows[v], found[part][v]) for v in range(VALUES)]
        return found

    stacks = []
    for found in gather([(over_s, subf), (over_s, subf + 8.0)]):
        pieces = [split(v) for v in found]
        stacks.append(jnp.concatenate([p[0] for p in pieces] + [p[1] for p in pieces], axis=0).astype(BF16))
    lanes = lax.broadcasted_iota(jnp.int32, (PEERS, PEERS), 0)
    ahead = jnp.where(lanes < lax.broadcasted_iota(jnp.int32, (PEERS, PEERS), 1), 1.0, 0.0).astype(BF16)
    start = jnp.dot(jnp.broadcast_to(left, (16, PEERS)).astype(BF16), ahead, preferred_element_type=F32)[0:1]
    picked = [jnp.zeros((8, PEERS), F32) for _ in range(VALUES)]
    for k in range(16):
        spot = jnp.where(jnp.logical_and(left > k, few), start + k, -1.0)
        moved = lax.dot_general(stacks[k // 8], hot(spot), NT, preferred_element_type=F32)
        for v in range(VALUES):
            value = moved[v * 8:v * 8 + 8] + moved[(VALUES + v) * 8:(VALUES + v) * 8 + 8]
            picked[v] = picked[v] + jnp.where(sub == k % 8, value, 0.0)
    picked = [jnp.sum(v, axis=0, keepdims=True) for v in picked]
    spot = picked[7].astype(jnp.int32)
    few_rows = rows_of(kernel_weights(picked[6]), ((spot >> 8) & 15).astype(F32), picked[:FIELDS])
    few_plane = (spot >> 12) & 7
    few_y = (spot & 255).astype(F32)

    pair = 2
    for step in range(PLANES // pair):
        found = gather([(to_s, subf + float((step * pair + part) * 8)) for part in range(pair)])
        for part in range(pair):
            spot = found[part][7].astype(jnp.int32)
            z = step * pair + part
            for v in range(FIELDS):
                mine_s[z, v] = found[part][v]
            mine_s[z, 6] = ((spot >> 8) & 15).astype(F32)
            mine_s[z, 7] = (spot & 255).astype(F32)
            for number, weight in enumerate(kernel_weights(found[part][6])):
                weight_s[z, number] = weight
    for z in range(PLANES):
        packed, ones = [few_rows], [hot(jnp.where(few_plane == z, few_y, -1.0))]
        for own in range(OWN):
            row = lambda v: mine_s[z, v, own:own + 1, :]
            packed.append(rows_of([weight_s[z, k, own:own + 1, :] for k in range(4)], row(6), [row(f) for f in range(FIELDS)]))
            ones.append(hot(row(7)))
        acc[z] = lax.dot_general(
            jnp.concatenate(ones, axis=1), jnp.concatenate(packed, axis=1), NT, preferred_element_type=F32
        )

    def extra_step(number, carry):
        hit = over_s[...] == number.astype(F32)
        pick = lambda v: jnp.sum(jnp.where(hit, flat_s[v * SLOTS:(v + 1) * SLOTS, :], 0.0), axis=0, keepdims=True)
        field = [pick(f) for f in range(FIELDS)]
        weights = kernel_weights(pick(6))
        spot = pick(7).astype(jnp.int32)
        packed = rows_of(weights, ((spot >> 8) & 15).astype(F32), field)
        plane = (spot >> 12) & 7
        spot_y = (spot & 255).astype(F32)
        for z in range(PLANES):
            acc[z] += lax.dot_general(hot(jnp.where(plane == z, spot_y, -1.0)), packed, NT, preferred_element_type=F32)
        return carry

    lax.fori_loop(0, rounds, extra_step, 0)
    for z in range(PLANES):
        nodes = jnp.swapaxes(acc[z, :, :128] + acc[z, :, 128:], 0, 1)
        for f in range(FIELDS):
            for half in range(2):
                at = (f * 2 + half) * 8
                lattice[f, half * 8:half * 8 + 8, z, :] = nodes[at:at + 8, :]
            at = 96 + f * 4
            low_edge[f, 0, z:z + 1, :] = nodes[at:at + 1, :]
            high_edge[f, 0, z:z + 1, :] = nodes[at + 1:at + 2, :]
            high_edge[f, 1, z:z + 1, :] = nodes[at + 2:at + 3, :]


def y_factors(y_offset, y_frac):
    weights = kernel_weights(y_frac)
    is_shift = [y_offset == s for s in range(-2, 3)]
    factors = []
    for travel in range(-3, 5):
        factor = jnp.zeros_like(weights[0])
        for s in range(-2, 3):
            if -1 <= travel - s <= 2:
                factor = jnp.where(is_shift[s + 2], weights[travel - s + 1], factor)
        factors.append(factor)
    return factors


def y_spread(values, factors):
    total = values * factors[3]
    for travel in range(-3, 5):
        if travel:
            total = total + pltpu.roll(values * factors[travel + 3], travel % values.shape[1], 1)
    return total


def y_inner_kernel(lattice, y_offset, y_frac, out, ready, sems):
    width = y_offset.shape[0]

    moves = []
    for x in range(2, width - 1):
        factors = y_factors(y_offset[x], y_frac[x])
        for f in range(FIELDS):
            ready[x, f] = y_spread(lattice[f, x], factors)
        moves.append(pltpu.make_async_copy(ready.at[x], out.at[:, x], sems.at[x]))
        moves[-1].start()
    for move in moves:
        move.wait()


def y_edge_kernel(lattice, from_right, from_left, y_offset, y_frac, partial, out, ready, sems):
    width = y_offset.shape[0]
    moves = []
    for number, (x, halo, at) in enumerate(((0, from_left, 0), (1, from_left, 1), (width - 1, from_right, 0))):
        factors = y_factors(y_offset[x], y_frac[x])
        for f in range(FIELDS):
            ready[f, number] = y_spread(lattice[f, x] + halo[f, at], factors)
        moves.append(pltpu.make_async_copy(ready.at[:, number], out.at[:, x], sems.at[number]))
        moves[-1].start()
    for move in moves:
        move.wait()


def params(mib):
    return pltpu.CompilerParams(vmem_limit_bytes=mib << 20)


def bucket(fields, frac, owner, slab, line_in, xcell, count):
    rows = frac.shape[0] // 128
    grid2 = lambda v: v.reshape(rows, 128)
    return pl.pallas_call(
        bucket_kernel,
        out_shape=jax.ShapeDtypeStruct((PEERS, 1, VALUES * SLOTS), F32),
        in_specs=[pl.BlockSpec(memory_space=pltpu.HBM)] * 7,
        scratch_shapes=[
            pltpu.VMEM(fields.shape, F32),
            pltpu.VMEM((rows, 128), F32),
            pltpu.VMEM((rows, 128), jnp.int32),
            pltpu.VMEM((rows, 128), jnp.int32),
            pltpu.VMEM((rows, 128), jnp.int32),
            pltpu.VMEM((rows, 128), jnp.int32),
            pltpu.VMEM((1, rows), jnp.int32),
            pltpu.SemaphoreType.DMA((7,)),
            pltpu.VMEM((rows, 128), F32),
            pltpu.VMEM((rows, 128), F32),
            pltpu.VMEM((4, rows, 128), F32),
            pltpu.VMEM((PEERS, rows * 128), BF16),
            pltpu.VMEM((PEERS, 128), BF16),
            pltpu.VMEM((2 * VALUES * SLOTS, PEERS), F32),
        ],
        compiler_params=params(56),
        name="bucket",
    )(fields, grid2(frac), grid2(owner), grid2(slab), grid2(line_in), grid2(xcell), count.reshape(1, rows))


def deposit(arrived):
    return pl.pallas_call(
        deposit_kernel,
        out_shape=(
            jax.ShapeDtypeStruct((FIELDS, 16, 8, 256), F32),
            jax.ShapeDtypeStruct((FIELDS, 1, 8, 256), F32),
            jax.ShapeDtypeStruct((FIELDS, 2, 8, 256), F32),
        ),
        scratch_shapes=[
            pltpu.VMEM((VALUES * SLOTS, PEERS), F32),
            pltpu.VMEM((SLOTS, PEERS), F32),
            pltpu.VMEM((SLOTS, PEERS), F32),
            pltpu.VMEM((SLOTS, PEERS), F32),
            pltpu.VMEM((PLANES, VALUES, 8, PEERS), F32),
            pltpu.VMEM((PLANES, 4, 8, PEERS), F32),
            pltpu.VMEM((8, 256, 256), F32),
        ],
        compiler_params=params(24),
        name="deposit",
    )(arrived)


def y_inner(lattice, y_offset, y_frac):
    return pl.pallas_call(
        y_inner_kernel,
        out_shape=jax.ShapeDtypeStruct(lattice.shape, F32),
        out_specs=pl.BlockSpec(memory_space=pltpu.HBM),
        scratch_shapes=[
            pltpu.VMEM((lattice.shape[1], FIELDS) + lattice.shape[2:], F32),
            pltpu.SemaphoreType.DMA((lattice.shape[1],)),
        ],
        compiler_params=params(16),
        cost_estimate=pl.CostEstimate(flops=20 * lattice.size, bytes_accessed=8 * lattice.size, transcendentals=0),
        name="y_inner",
    )(lattice, y_offset, y_frac)


def y_edge(lattice, from_right, from_left, y_offset, y_frac, partial):
    vmem = pl.BlockSpec(memory_space=pltpu.VMEM)
    return pl.pallas_call(
        y_edge_kernel,
        out_shape=jax.ShapeDtypeStruct(lattice.shape, F32),
        in_specs=[vmem] * 5 + [pl.BlockSpec(memory_space=pltpu.HBM)],
        out_specs=pl.BlockSpec(memory_space=pltpu.HBM),
        input_output_aliases={5: 0},
        scratch_shapes=[
            pltpu.VMEM((FIELDS, 3) + lattice.shape[2:], F32),
            pltpu.SemaphoreType.DMA((3,)),
        ],
        compiler_params=params(16),
        name="y_edge",
    )(lattice, from_right, from_left, y_offset, y_frac, partial)


def per_device(fields, frac_x, owner, slab, line_in, xcell, tile_count, y_offset, y_frac):
    lines = lax.axis_size("lines")
    outgoing = bucket(fields, frac_x, owner, slab, line_in, xcell, tile_count)
    arrived = lax.all_to_all(outgoing, ("lines", "slab"), split_axis=0, concat_axis=0, tiled=True)
    lattice, low_edge, high_edge = deposit(arrived)
    from_left = lax.ppermute(high_edge, "lines", [(i, (i + 1) % lines) for i in range(lines)])
    from_right = lax.ppermute(low_edge, "lines", [(i, (i - 1) % lines) for i in range(lines)])
    partial = y_inner(lattice, y_offset, y_frac)
    return y_edge(lattice, from_right, from_left, y_offset, y_frac, partial)


def solution(mesh):
    return jax.shard_map(
        per_device,
        mesh=mesh,
        in_specs=(
            P(None, ("lines", "slab")),
            P(("lines", "slab")),
            P(("lines", "slab")),
            P(("lines", "slab")),
            P(("lines", "slab")),
            P(("lines", "slab")),
            P(("lines", "slab")),
            P("lines", "slab", None),
            P("lines", "slab", None),
        ),
        out_specs=P(None, "lines", "slab", None),
        check_vma=False,
    )
```

```python
import functools

import jax
import jax.numpy as jnp
from jax import lax
from jax.experimental import pallas as pl
from jax.experimental.pallas import tpu as pltpu
from jax.sharding import PartitionSpec as P

F32 = jnp.float32
BF16 = jnp.bfloat16
NT = (((1,), (1,)), ((), ()))

FIELDS = 6
SLOTS = 48
VALUES = 8
PEERS = 256
PLANES = 8
OWN = 6


def kernel_weights(offset):
    remain = 1.0 - offset
    return (
        -0.5 * offset * remain * remain,
        1.0 - 2.5 * offset * offset + 1.5 * offset * offset * offset,
        1.0 - 2.5 * remain * remain + 1.5 * remain * remain * remain,
        -0.5 * offset * offset * remain,
    )


def split(value):
    high = value.astype(BF16).astype(F32)
    return high, (value - high).astype(BF16).astype(F32)


def bucket_kernel(
    fields_h, frac_h, owner_h, slab_h, line_in_h, xcell_h, count_h, out,
    fields, frac, owner, slab, line_in, xcell, count, sems, key_s, rank_s, place_s, hot_s, hist_s, acc,
):
    moves = [
        pltpu.make_async_copy(source, goal, sems.at[number])
        for number, (source, goal) in enumerate((
            (count_h, count), (slab_h, slab), (xcell_h, xcell), (owner_h, owner), (line_in_h, line_in), (frac_h, frac),
            (fields_h, fields),
        ))
    ]
    for move in moves:
        move.start()
    for move in moves[:3]:
        move.wait()
    rows = key_s.shape[0]
    lane = lax.broadcasted_iota(jnp.int32, key_s.shape, 1)
    tile = lax.broadcasted_iota(jnp.int32, (rows, rows), 0) == lax.broadcasted_iota(jnp.int32, (rows, rows), 1)
    alive = lane < jnp.sum(jnp.where(tile, count[...], 0), axis=1, keepdims=True)
    key_s[...] = jnp.where(alive, (xcell[...] >> 4) * 8 + slab[...], -1).astype(F32)
    sixteen = lax.broadcasted_iota(jnp.int32, (16, 128), 0).astype(F32)
    one, zero = jnp.ones((), BF16), jnp.zeros((), BF16)

    def wide_row(row):
        return jnp.broadcast_to(row, (16, 128)).astype(BF16)

    total = jnp.zeros((PEERS, 128), BF16)
    for row in range(rows):
        key = wide_row(key_s[row:row + 1, :])
        hot = jnp.concatenate(
            [jnp.where(key == (sixteen + 16.0 * g).astype(BF16), one, zero) for g in range(PEERS // 16)], axis=0
        )
        hot_s[:, row * 128:row * 128 + 128] = hot
        total = total + hot
    earlier = lax.broadcasted_iota(jnp.int32, (128, 128), 0) < lax.broadcasted_iota(jnp.int32, (128, 128), 1)
    base = jnp.dot(total, jnp.where(earlier, 1.0, 0.0).astype(BF16), preferred_element_type=F32)
    hist_s[...] = base.astype(BF16)
    sub = lax.broadcasted_iota(jnp.int32, (8, 128), 0)
    groups = rows // 8
    keys = [key_s[g * 8:g * 8 + 8, :] for g in range(groups)]
    above = [jnp.zeros((8, 128), F32) for _ in range(groups)]
    for row in range(rows):
        key = key_s[row:row + 1, :]
        for g in range(row // 8, groups):
            same = keys[g] == key
            if g == row // 8:
                same = jnp.logical_and(same, sub > row % 8)
            above[g] = above[g] + jnp.where(same, 1.0, 0.0)
    for g in range(groups):
        rank_s[g * 8:g * 8 + 8, :] = above[g]

    for move in moves[3:]:
        move.wait()
    place_s[0] = (owner[...] * 8 + (line_in[...] >> 3)).astype(F32)
    place_s[1] = ((128 + (line_in[...] & 7) * 16 + (xcell[...] & 15)) * 256).astype(F32)
    place_s[2], place_s[3] = split(frac[...])
    wide = 8
    acc[...] = jnp.zeros_like(acc)

    for step in range(rows // wide):
        packed = []
        for part in range(wide):
            row = step * wide + part
            columns = pl.ds(row * 128, 128)
            seen = hot_s[:, columns] * hist_s[...]
            some = seen[0:16]
            for g in range(1, PEERS // 16):
                some = some + seen[g * 16:g * 16 + 16]
            rank = jnp.sum(some.astype(F32), axis=0, keepdims=True) + rank_s[row:row + 1, :]
            rank = wide_row(rank)
            here = [rank == (sixteen + 16.0 * g).astype(BF16) for g in range(SLOTS // 16)]
            high, low = split(fields[:, columns])
            highs = [high[f:f + 1] for f in range(FIELDS)]
            lows = [low[f:f + 1] for f in range(FIELDS)]
            highs += [place_s[2, row:row + 1, :], place_s[0, row:row + 1, :]]
            lows += [place_s[3, row:row + 1, :], place_s[1, row:row + 1, :]]
            pieces = []
            for v in highs + lows:
                v = wide_row(v)
                pieces += [jnp.where(h, v, zero) for h in here]
            packed.append(jnp.concatenate(pieces, axis=0))
        block = hot_s[:, pl.ds(step * wide * 128, wide * 128)]
        acc[...] += lax.dot_general(jnp.concatenate(packed, axis=1), block, NT, preferred_element_type=F32)
    half = VALUES * SLOTS
    total = acc[:half, :] + acc[half:, :]
    out[...] = jnp.swapaxes(total, 0, 1)[:, None, :]


def deposit_kernel(arrived, lattice, low_edge, high_edge, flat_s, plane_s, to_s, over_s, mine_s, weight_s, acc):
    flat_s[...] = jnp.swapaxes(arrived[:, 0, :], 0, 1)
    place = flat_s[7 * SLOTS:8 * SLOTS, :].astype(jnp.int32)
    live = place >= 32768
    plane = jnp.where(live, (place >> 12) & 7, 99).astype(F32)
    plane_s[...] = plane
    sub = lax.broadcasted_iota(jnp.int32, (8, PEERS), 0)
    subf = sub.astype(F32)
    seen = jnp.zeros((PLANES, PEERS), F32)
    for slot in range(SLOTS):
        hit = plane_s[slot:slot + 1, :] == subf
        to_s[slot:slot + 1, :] = jnp.sum(jnp.where(hit, seen, 0.0), axis=0, keepdims=True)
        seen = seen + jnp.where(hit, 1.0, 0.0)
    rank = to_s[...]
    fits = rank < OWN
    to_s[...] = jnp.where(fits, plane * 8 + rank, 9999.0)
    extra = jnp.logical_and(live, jnp.logical_not(fits))
    before = lax.broadcasted_iota(jnp.int32, (SLOTS, SLOTS), 1) < lax.broadcasted_iota(jnp.int32, (SLOTS, SLOTS), 0)
    order = jnp.dot(jnp.where(before, 1.0, 0.0).astype(BF16), jnp.where(extra, 1.0, 0.0).astype(BF16), preferred_element_type=F32)
    over_s[...] = jnp.where(extra, order, -1.0)
    left = jnp.sum(jnp.maximum(seen - OWN, 0.0), axis=0, keepdims=True)
    most = jnp.max(left, axis=1, keepdims=True)
    few = jnp.logical_and(jnp.sum(left, axis=1, keepdims=True) <= PEERS, most <= 16)
    rounds = jnp.max(jnp.where(few, 0.0, most)).astype(jnp.int32)

    low_rows = (sub + 1).astype(F32)
    high_rows = (sub + 9).astype(F32)
    edge_rows = jnp.where(sub % 4 == 0, 0, jnp.where(sub % 4 == 3, 99, 16 + sub % 4)).astype(F32)
    first = sub < 4
    sixteen = lax.broadcasted_iota(jnp.int32, (16, PEERS), 0).astype(F32)
    levels = [(sixteen + 16.0 * g).astype(BF16) for g in range(16)]

    one, zero = jnp.ones((), BF16), jnp.zeros((), BF16)

    def hot(row):
        row = jnp.broadcast_to(row, (16, PEERS)).astype(BF16)
        return jnp.concatenate([jnp.where(row == level, one, zero) for level in levels], axis=0)

    def rows_of(weights, xin, field):
        spread = []
        for nodes in (low_rows, high_rows, edge_rows):
            apart = nodes - xin
            value = jnp.zeros((8, PEERS), F32)
            for k in range(4):
                value = jnp.where(apart == float(k), weights[k], value)
            spread.append(value)
        groups = []
        for f in range(FIELDS):
            groups += [spread[0] * field[f], spread[1] * field[f]]
        for f in range(0, FIELDS, 2):
            groups.append(spread[2] * jnp.where(first, field[f], field[f + 1]))
        groups.append(jnp.zeros((8, PEERS), F32))
        whole = jnp.concatenate(groups, axis=0)
        high = whole.astype(BF16)
        low = (whole - high.astype(F32)).astype(BF16)
        return jnp.concatenate([high, low], axis=0)

    def gather(goals):
        found = [[jnp.zeros((8, PEERS), F32) for _ in range(VALUES)] for _ in goals]
        for slot in range(SLOTS):
            rows = [flat_s[v * SLOTS + slot:v * SLOTS + slot + 1, :] for v in range(VALUES)]
            for part, (numbers, goal) in enumerate(goals):
                hit = numbers[slot:slot + 1, :] == goal
                found[part] = [jnp.where(hit, rows[v], found[part][v]) for v in range(VALUES)]
        return found

    stacks = []
    for found in gather([(over_s, subf), (over_s, subf + 8.0)]):
        pieces = [split(v) for v in found]
        stacks.append(jnp.concatenate([p[0] for p in pieces] + [p[1] for p in pieces], axis=0).astype(BF16))
    lanes = lax.broadcasted_iota(jnp.int32, (PEERS, PEERS), 0)
    ahead = jnp.where(lanes < lax.broadcasted_iota(jnp.int32, (PEERS, PEERS), 1), 1.0, 0.0).astype(BF16)
    start = jnp.dot(jnp.broadcast_to(left, (16, PEERS)).astype(BF16), ahead, preferred_element_type=F32)[0:1]
    picked = [jnp.zeros((8, PEERS), F32) for _ in range(VALUES)]
    for k in range(16):
        spot = jnp.where(jnp.logical_and(left > k, few), start + k, -1.0)
        moved = lax.dot_general(stacks[k // 8], hot(spot), NT, preferred_element_type=F32)
        for v in range(VALUES):
            value = moved[v * 8:v * 8 + 8] + moved[(VALUES + v) * 8:(VALUES + v) * 8 + 8]
            picked[v] = picked[v] + jnp.where(sub == k % 8, value, 0.0)
    picked = [jnp.sum(v, axis=0, keepdims=True) for v in picked]
    spot = picked[7].astype(jnp.int32)
    few_rows = rows_of(kernel_weights(picked[6]), ((spot >> 8) & 15).astype(F32), picked[:FIELDS])
    few_plane = (spot >> 12) & 7
    few_y = (spot & 255).astype(F32)

    pair = 2
    for step in range(PLANES // pair):
        found = gather([(to_s, subf + float((step * pair + part) * 8)) for part in range(pair)])
        for part in range(pair):
            spot = found[part][7].astype(jnp.int32)
            z = step * pair + part
            for v in range(FIELDS):
                mine_s[z, v] = found[part][v]
            mine_s[z, 6] = ((spot >> 8) & 15).astype(F32)
            mine_s[z, 7] = (spot & 255).astype(F32)
            for number, weight in enumerate(kernel_weights(found[part][6])):
                weight_s[z, number] = weight
    for z in range(PLANES):
        packed, ones = [few_rows], [hot(jnp.where(few_plane == z, few_y, -1.0))]
        for own in range(OWN):
            row = lambda v: mine_s[z, v, own:own + 1, :]
            packed.append(rows_of([weight_s[z, k, own:own + 1, :] for k in range(4)], row(6), [row(f) for f in range(FIELDS)]))
            ones.append(hot(row(7)))
        acc[z] = lax.dot_general(
            jnp.concatenate(ones, axis=1), jnp.concatenate(packed, axis=1), NT, preferred_element_type=F32
        )

    def extra_step(number, carry):
        hit = over_s[...] == number.astype(F32)
        pick = lambda v: jnp.sum(jnp.where(hit, flat_s[v * SLOTS:(v + 1) * SLOTS, :], 0.0), axis=0, keepdims=True)
        field = [pick(f) for f in range(FIELDS)]
        weights = kernel_weights(pick(6))
        spot = pick(7).astype(jnp.int32)
        packed = rows_of(weights, ((spot >> 8) & 15).astype(F32), field)
        plane = (spot >> 12) & 7
        spot_y = (spot & 255).astype(F32)
        for z in range(PLANES):
            acc[z] += lax.dot_general(hot(jnp.where(plane == z, spot_y, -1.0)), packed, NT, preferred_element_type=F32)
        return carry

    lax.fori_loop(0, rounds, extra_step, 0)
    low_edge[:, 1] = jnp.zeros((FIELDS,) + low_edge.shape[2:], F32)
    for z in range(PLANES):
        nodes = jnp.swapaxes(acc[z, :, :128] + acc[z, :, 128:], 0, 1)
        for f in range(FIELDS):
            for half in range(2):
                at = (f * 2 + half) * 8
                lattice[f, half * 8:half * 8 + 8, z, :] = nodes[at:at + 8, :]
            at = 96 + f * 4
            low_edge[f, 0, z:z + 1, :] = nodes[at:at + 1, :]
            high_edge[f, 0, z:z + 1, :] = nodes[at + 1:at + 2, :]
            high_edge[f, 1, z:z + 1, :] = nodes[at + 2:at + 3, :]


def y_factors(y_offset, y_frac):
    weights = kernel_weights(y_frac)
    is_shift = [y_offset == s for s in range(-2, 3)]
    factors = []
    for travel in range(-3, 5):
        factor = jnp.zeros_like(weights[0])
        for s in range(-2, 3):
            if -1 <= travel - s <= 2:
                factor = jnp.where(is_shift[s + 2], weights[travel - s + 1], factor)
        factors.append(factor)
    return factors


def y_spread(values, factors):
    total = values * factors[3]
    for travel in range(-3, 5):
        if travel:
            total = total + pltpu.roll(values * factors[travel + 3], travel % values.shape[1], 1)
    return total


def y_inner_kernel(lattice, y_offset, y_frac, out, ready, sems):
    width = y_offset.shape[0]

    moves = []
    for x in range(2, width - 1):
        factors = y_factors(y_offset[x], y_frac[x])
        for f in range(FIELDS):
            ready[x, f] = y_spread(lattice[f, x], factors)
        moves.append(pltpu.make_async_copy(ready.at[x], out.at[:, x], sems.at[x]))
        moves[-1].start()
    for move in moves:
        move.wait()


def y_edge_kernel(lattice, from_right, from_left, y_offset, y_frac, partial, out, ready, sems):
    width = y_offset.shape[0]
    moves = []
    for number, (x, halo, at) in enumerate(((0, from_left, 0), (1, from_left, 1), (width - 1, from_right, 0))):
        factors = y_factors(y_offset[x], y_frac[x])
        for f in range(FIELDS):
            ready[f, number] = y_spread(lattice[f, x] + halo[f, at], factors)
        moves.append(pltpu.make_async_copy(ready.at[:, number], out.at[:, x], sems.at[number]))
        moves[-1].start()
    for move in moves:
        move.wait()


def params(mib):
    return pltpu.CompilerParams(vmem_limit_bytes=mib << 20)


def bucket(fields, frac, owner, slab, line_in, xcell, count):
    rows = frac.shape[0] // 128
    grid2 = lambda v: v.reshape(rows, 128)
    return pl.pallas_call(
        bucket_kernel,
        out_shape=jax.ShapeDtypeStruct((PEERS, 1, VALUES * SLOTS), F32),
        in_specs=[pl.BlockSpec(memory_space=pltpu.HBM)] * 7,
        scratch_shapes=[
            pltpu.VMEM(fields.shape, F32),
            pltpu.VMEM((rows, 128), F32),
            pltpu.VMEM((rows, 128), jnp.int32),
            pltpu.VMEM((rows, 128), jnp.int32),
            pltpu.VMEM((rows, 128), jnp.int32),
            pltpu.VMEM((rows, 128), jnp.int32),
            pltpu.VMEM((1, rows), jnp.int32),
            pltpu.SemaphoreType.DMA((7,)),
            pltpu.VMEM((rows, 128), F32),
            pltpu.VMEM((rows, 128), F32),
            pltpu.VMEM((4, rows, 128), F32),
            pltpu.VMEM((PEERS, rows * 128), BF16),
            pltpu.VMEM((PEERS, 128), BF16),
            pltpu.VMEM((2 * VALUES * SLOTS, PEERS), F32),
        ],
        compiler_params=params(56),
        name="bucket",
    )(fields, grid2(frac), grid2(owner), grid2(slab), grid2(line_in), grid2(xcell), count.reshape(1, rows))


def deposit(arrived):
    return pl.pallas_call(
        deposit_kernel,
        out_shape=(
            jax.ShapeDtypeStruct((FIELDS, 16, 8, 256), F32),
            jax.ShapeDtypeStruct((FIELDS, 2, 8, 256), F32),
            jax.ShapeDtypeStruct((FIELDS, 2, 8, 256), F32),
        ),
        scratch_shapes=[
            pltpu.VMEM((VALUES * SLOTS, PEERS), F32),
            pltpu.VMEM((SLOTS, PEERS), F32),
            pltpu.VMEM((SLOTS, PEERS), F32),
            pltpu.VMEM((SLOTS, PEERS), F32),
            pltpu.VMEM((PLANES, VALUES, 8, PEERS), F32),
            pltpu.VMEM((PLANES, 4, 8, PEERS), F32),
            pltpu.VMEM((8, 256, 256), F32),
        ],
        compiler_params=params(24),
        name="deposit",
    )(arrived)


def y_inner(lattice, y_offset, y_frac):
    return pl.pallas_call(
        y_inner_kernel,
        out_shape=jax.ShapeDtypeStruct(lattice.shape, F32),
        out_specs=pl.BlockSpec(memory_space=pltpu.HBM),
        scratch_shapes=[
            pltpu.VMEM((lattice.shape[1], FIELDS) + lattice.shape[2:], F32),
            pltpu.SemaphoreType.DMA((lattice.shape[1],)),
        ],
        compiler_params=params(16),
        cost_estimate=pl.CostEstimate(flops=20 * lattice.size, bytes_accessed=8 * lattice.size, transcendentals=0),
        name="y_inner",
    )(lattice, y_offset, y_frac)


def y_edge(lattice, from_right, from_left, y_offset, y_frac, partial):
    vmem = pl.BlockSpec(memory_space=pltpu.VMEM)
    return pl.pallas_call(
        y_edge_kernel,
        out_shape=jax.ShapeDtypeStruct(lattice.shape, F32),
        in_specs=[vmem] * 5 + [pl.BlockSpec(memory_space=pltpu.HBM)],
        out_specs=pl.BlockSpec(memory_space=pltpu.HBM),
        input_output_aliases={5: 0},
        scratch_shapes=[
            pltpu.VMEM((FIELDS, 3) + lattice.shape[2:], F32),
            pltpu.SemaphoreType.DMA((3,)),
        ],
        compiler_params=params(16),
        name="y_edge",
    )(lattice, from_right, from_left, y_offset, y_frac, partial)


def per_device(fields, frac_x, owner, slab, line_in, xcell, tile_count, y_offset, y_frac):
    lines = lax.axis_size("lines")
    outgoing = bucket(fields, frac_x, owner, slab, line_in, xcell, tile_count)
    arrived = lax.all_to_all(outgoing, ("lines", "slab"), split_axis=0, concat_axis=0, tiled=True)
    lattice, low_edge, high_edge = deposit(arrived)
    from_left = lax.ppermute(high_edge, "lines", [(i, (i + 1) % lines) for i in range(lines)])
    from_right = lax.ppermute(low_edge, "lines", [(i, (i - 1) % lines) for i in range(lines)])
    partial = y_inner(lattice, y_offset, y_frac)
    return y_edge(lattice, from_right, from_left, y_offset, y_frac, partial)


def solution(mesh):
    return jax.shard_map(
        per_device,
        mesh=mesh,
        in_specs=(
            P(None, ("lines", "slab")),
            P(("lines", "slab")),
            P(("lines", "slab")),
            P(("lines", "slab")),
            P(("lines", "slab")),
            P(("lines", "slab")),
            P(("lines", "slab")),
            P("lines", "slab", None),
            P("lines", "slab", None),
        ),
        out_specs=P(None, "lines", "slab", None),
        check_vma=False,
    )
```

```python
import functools

import jax
import jax.numpy as jnp
from jax import lax
from jax.experimental import pallas as pl
from jax.experimental.pallas import tpu as pltpu
from jax.sharding import PartitionSpec as P

F32 = jnp.float32
BF16 = jnp.bfloat16
NT = (((1,), (1,)), ((), ()))

FIELDS = 6
SLOTS = 48
VALUES = 8
PEERS = 256
PLANES = 8
OWN = 6


def kernel_weights(offset):
    remain = 1.0 - offset
    return (
        -0.5 * offset * remain * remain,
        1.0 - 2.5 * offset * offset + 1.5 * offset * offset * offset,
        1.0 - 2.5 * remain * remain + 1.5 * remain * remain * remain,
        -0.5 * offset * offset * remain,
    )


def split(value):
    high = value.astype(BF16).astype(F32)
    return high, (value - high).astype(BF16).astype(F32)


def bucket_kernel(
    fields_h, frac_h, owner_h, slab_h, line_in_h, xcell_h, count_h, out,
    fields, frac, owner, slab, line_in, xcell, count, sems, key_s, rank_s, place_s, hot_s, hist_s, acc,
):
    moves = [
        pltpu.make_async_copy(source, goal, sems.at[number])
        for number, (source, goal) in enumerate((
            (count_h, count), (slab_h, slab), (xcell_h, xcell), (owner_h, owner), (line_in_h, line_in), (frac_h, frac),
            (fields_h, fields),
        ))
    ]
    for move in moves:
        move.start()
    for move in moves[:3]:
        move.wait()
    rows = key_s.shape[0]
    lane = lax.broadcasted_iota(jnp.int32, key_s.shape, 1)
    tile = lax.broadcasted_iota(jnp.int32, (rows, rows), 0) == lax.broadcasted_iota(jnp.int32, (rows, rows), 1)
    alive = lane < jnp.sum(jnp.where(tile, count[...], 0), axis=1, keepdims=True)
    key_s[...] = jnp.where(alive, (xcell[...] >> 4) * 8 + slab[...], -1).astype(F32)
    sixteen = lax.broadcasted_iota(jnp.int32, (16, 128), 0).astype(F32)
    one, zero = jnp.ones((), BF16), jnp.zeros((), BF16)

    def wide_row(row):
        return jnp.broadcast_to(row, (16, 128)).astype(BF16)

    total = jnp.zeros((PEERS, 128), BF16)
    for row in range(rows):
        key = wide_row(key_s[row:row + 1, :])
        hot = jnp.concatenate(
            [jnp.where(key == (sixteen + 16.0 * g).astype(BF16), one, zero) for g in range(PEERS // 16)], axis=0
        )
        hot_s[:, row * 128:row * 128 + 128] = hot
        total = total + hot
    earlier = lax.broadcasted_iota(jnp.int32, (128, 128), 0) < lax.broadcasted_iota(jnp.int32, (128, 128), 1)
    base = jnp.dot(total, jnp.where(earlier, 1.0, 0.0).astype(BF16), preferred_element_type=F32)
    hist_s[...] = base.astype(BF16)
    sub = lax.broadcasted_iota(jnp.int32, (8, 128), 0)
    groups = rows // 8
    keys = [key_s[g * 8:g * 8 + 8, :] for g in range(groups)]
    above = [jnp.zeros((8, 128), F32) for _ in range(groups)]
    for row in range(rows):
        key = key_s[row:row + 1, :]
        for g in range(row // 8, groups):
            same = keys[g] == key
            if g == row // 8:
                same = jnp.logical_and(same, sub > row % 8)
            above[g] = above[g] + jnp.where(same, 1.0, 0.0)
    for g in range(groups):
        rank_s[g * 8:g * 8 + 8, :] = above[g]

    for move in moves[3:]:
        move.wait()
    place_s[0] = (owner[...] * 8 + (line_in[...] >> 3)).astype(F32)
    place_s[1] = ((128 + (line_in[...] & 7) * 16 + (xcell[...] & 15)) * 256).astype(F32)
    place_s[2], place_s[3] = split(frac[...])
    wide = 8
    acc[...] = jnp.zeros_like(acc)

    for step in range(rows // wide):
        packed = []
        for part in range(wide):
            row = step * wide + part
            columns = pl.ds(row * 128, 128)
            seen = hot_s[:, columns] * hist_s[...]
            some = seen[0:16]
            for g in range(1, PEERS // 16):
                some = some + seen[g * 16:g * 16 + 16]
            rank = jnp.sum(some.astype(F32), axis=0, keepdims=True) + rank_s[row:row + 1, :]
            rank = wide_row(rank)
            here = [rank == (sixteen + 16.0 * g).astype(BF16) for g in range(SLOTS // 16)]
            high, low = split(fields[:, columns])
            highs = [high[f:f + 1] for f in range(FIELDS)]
            lows = [low[f:f + 1] for f in range(FIELDS)]
            highs += [place_s[2, row:row + 1, :], place_s[0, row:row + 1, :]]
            lows += [place_s[3, row:row + 1, :], place_s[1, row:row + 1, :]]
            pieces = []
            for v in highs + lows:
                v = wide_row(v)
                pieces += [jnp.where(h, v, zero) for h in here]
            packed.append(jnp.concatenate(pieces, axis=0))
        block = hot_s[:, pl.ds(step * wide * 128, wide * 128)]
        acc[...] += lax.dot_general(jnp.concatenate(packed, axis=1), block, NT, preferred_element_type=F32)
    half = VALUES * SLOTS
    total = acc[:half, :] + acc[half:, :]
    out[...] = jnp.swapaxes(total, 0, 1)[:, None, :]


def deposit_kernel(arrived, lattice, low_edge, high_edge, flat_s, plane_s, to_s, over_s, mine_s, weight_s, acc):
    flat_s[...] = jnp.swapaxes(arrived[:, 0, :], 0, 1)
    place = flat_s[7 * SLOTS:8 * SLOTS, :].astype(jnp.int32)
    live = place >= 32768
    plane = jnp.where(live, (place >> 12) & 7, 99).astype(F32)
    plane_s[...] = plane
    sub = lax.broadcasted_iota(jnp.int32, (8, PEERS), 0)
    subf = sub.astype(F32)
    seen = jnp.zeros((PLANES, PEERS), F32)
    for slot in range(SLOTS):
        hit = plane_s[slot:slot + 1, :] == subf
        to_s[slot:slot + 1, :] = jnp.sum(jnp.where(hit, seen, 0.0), axis=0, keepdims=True)
        seen = seen + jnp.where(hit, 1.0, 0.0)
    rank = to_s[...]
    fits = rank < OWN
    to_s[...] = jnp.where(fits, plane * 8 + rank, 9999.0)
    extra = jnp.logical_and(live, jnp.logical_not(fits))
    before = lax.broadcasted_iota(jnp.int32, (SLOTS, SLOTS), 1) < lax.broadcasted_iota(jnp.int32, (SLOTS, SLOTS), 0)
    order = jnp.dot(jnp.where(before, 1.0, 0.0).astype(BF16), jnp.where(extra, 1.0, 0.0).astype(BF16), preferred_element_type=F32)
    over_s[...] = jnp.where(extra, order, -1.0)
    left = jnp.sum(jnp.maximum(seen - OWN, 0.0), axis=0, keepdims=True)
    most = jnp.max(left, axis=1, keepdims=True)
    tiled = jnp.minimum(left, 16.0)
    few = jnp.sum(tiled, axis=1, keepdims=True) <= PEERS
    first_round = jnp.max(jnp.where(few, 16.0, 0.0)).astype(jnp.int32)
    last_round = jnp.max(most).astype(jnp.int32)

    low_rows = (sub + 1).astype(F32)
    high_rows = (sub + 9).astype(F32)
    edge_rows = jnp.where(sub % 4 == 0, 0, jnp.where(sub % 4 == 3, 99, 16 + sub % 4)).astype(F32)
    first = sub < 4
    sixteen = lax.broadcasted_iota(jnp.int32, (16, PEERS), 0).astype(F32)
    levels = [(sixteen + 16.0 * g).astype(BF16) for g in range(16)]

    one, zero = jnp.ones((), BF16), jnp.zeros((), BF16)

    def hot(row):
        row = jnp.broadcast_to(row, (16, PEERS)).astype(BF16)
        return jnp.concatenate([jnp.where(row == level, one, zero) for level in levels], axis=0)

    def rows_of(weights, xin, field):
        spread = []
        for nodes in (low_rows, high_rows, edge_rows):
            apart = nodes - xin
            value = jnp.zeros((8, PEERS), F32)
            for k in range(4):
                value = jnp.where(apart == float(k), weights[k], value)
            spread.append(value)
        groups = []
        for f in range(FIELDS):
            groups += [spread[0] * field[f], spread[1] * field[f]]
        for f in range(0, FIELDS, 2):
            groups.append(spread[2] * jnp.where(first, field[f], field[f + 1]))
        groups.append(jnp.zeros((8, PEERS), F32))
        whole = jnp.concatenate(groups, axis=0)
        high = whole.astype(BF16)
        low = (whole - high.astype(F32)).astype(BF16)
        return jnp.concatenate([high, low], axis=0)

    def gather(goals):
        found = [[jnp.zeros((8, PEERS), F32) for _ in range(VALUES)] for _ in goals]
        for slot in range(SLOTS):
            rows = [flat_s[v * SLOTS + slot:v * SLOTS + slot + 1, :] for v in range(VALUES)]
            for part, (numbers, goal) in enumerate(goals):
                hit = numbers[slot:slot + 1, :] == goal
                found[part] = [jnp.where(hit, rows[v], found[part][v]) for v in range(VALUES)]
        return found

    stacks = []
    for found in gather([(over_s, subf), (over_s, subf + 8.0)]):
        pieces = [split(v) for v in found]
        stacks.append(jnp.concatenate([p[0] for p in pieces] + [p[1] for p in pieces], axis=0).astype(BF16))
    lanes = lax.broadcasted_iota(jnp.int32, (PEERS, PEERS), 0)
    ahead = jnp.where(lanes < lax.broadcasted_iota(jnp.int32, (PEERS, PEERS), 1), 1.0, 0.0).astype(BF16)
    start = jnp.dot(jnp.broadcast_to(tiled, (16, PEERS)).astype(BF16), ahead, preferred_element_type=F32)[0:1]
    picked = [jnp.zeros((8, PEERS), F32) for _ in range(VALUES)]
    for k in range(16):
        spot = jnp.where(jnp.logical_and(left > k, few), start + k, -1.0)
        moved = lax.dot_general(stacks[k // 8], hot(spot), NT, preferred_element_type=F32)
        for v in range(VALUES):
            value = moved[v * 8:v * 8 + 8] + moved[(VALUES + v) * 8:(VALUES + v) * 8 + 8]
            picked[v] = picked[v] + jnp.where(sub == k % 8, value, 0.0)
    picked = [jnp.sum(v, axis=0, keepdims=True) for v in picked]
    spot = picked[7].astype(jnp.int32)
    few_rows = rows_of(kernel_weights(picked[6]), ((spot >> 8) & 15).astype(F32), picked[:FIELDS])
    few_plane = (spot >> 12) & 7
    few_y = (spot & 255).astype(F32)

    pair = 2
    for step in range(PLANES // pair):
        found = gather([(to_s, subf + float((step * pair + part) * 8)) for part in range(pair)])
        for part in range(pair):
            spot = found[part][7].astype(jnp.int32)
            z = step * pair + part
            for v in range(FIELDS):
                mine_s[z, v] = found[part][v]
            mine_s[z, 6] = ((spot >> 8) & 15).astype(F32)
            mine_s[z, 7] = (spot & 255).astype(F32)
            for number, weight in enumerate(kernel_weights(found[part][6])):
                weight_s[z, number] = weight
    for z in range(PLANES):
        packed, ones = [few_rows], [hot(jnp.where(few_plane == z, few_y, -1.0))]
        for own in range(OWN):
            row = lambda v: mine_s[z, v, own:own + 1, :]
            packed.append(rows_of([weight_s[z, k, own:own + 1, :] for k in range(4)], row(6), [row(f) for f in range(FIELDS)]))
            ones.append(hot(row(7)))
        acc[z] = lax.dot_general(
            jnp.concatenate(ones, axis=1), jnp.concatenate(packed, axis=1), NT, preferred_element_type=F32
        )

    def extra_step(number, carry):
        hit = over_s[...] == number.astype(F32)
        pick = lambda v: jnp.sum(jnp.where(hit, flat_s[v * SLOTS:(v + 1) * SLOTS, :], 0.0), axis=0, keepdims=True)
        field = [pick(f) for f in range(FIELDS)]
        weights = kernel_weights(pick(6))
        spot = pick(7).astype(jnp.int32)
        packed = rows_of(weights, ((spot >> 8) & 15).astype(F32), field)
        plane = (spot >> 12) & 7
        spot_y = (spot & 255).astype(F32)
        for z in range(PLANES):
            acc[z] += lax.dot_general(hot(jnp.where(plane == z, spot_y, -1.0)), packed, NT, preferred_element_type=F32)
        return carry

    lax.fori_loop(first_round, last_round, extra_step, 0)
    low_edge[:, 1] = jnp.zeros((FIELDS,) + low_edge.shape[2:], F32)
    for z in range(PLANES):
        nodes = jnp.swapaxes(acc[z, :, :128] + acc[z, :, 128:], 0, 1)
        for f in range(FIELDS):
            for half in range(2):
                at = (f * 2 + half) * 8
                lattice[f, half * 8:half * 8 + 8, z, :] = nodes[at:at + 8, :]
            at = 96 + f * 4
            low_edge[f, 0, z:z + 1, :] = nodes[at:at + 1, :]
            high_edge[f, 0, z:z + 1, :] = nodes[at + 1:at + 2, :]
            high_edge[f, 1, z:z + 1, :] = nodes[at + 2:at + 3, :]


def y_factors(y_offset, y_frac):
    weights = kernel_weights(y_frac)
    is_shift = [y_offset == s for s in range(-2, 3)]
    factors = []
    for travel in range(-3, 5):
        factor = jnp.zeros_like(weights[0])
        for s in range(-2, 3):
            if -1 <= travel - s <= 2:
                factor = jnp.where(is_shift[s + 2], weights[travel - s + 1], factor)
        factors.append(factor)
    return factors


def y_spread(values, factors):
    total = values * factors[3]
    for travel in range(-3, 5):
        if travel:
            total = total + pltpu.roll(values * factors[travel + 3], travel % values.shape[1], 1)
    return total


def y_inner_kernel(lattice, y_offset, y_frac, out, ready, sems):
    width = y_offset.shape[0]

    moves = []
    for x in range(2, width - 1):
        factors = y_factors(y_offset[x], y_frac[x])
        for f in range(FIELDS):
            ready[x, f] = y_spread(lattice[f, x], factors)
        moves.append(pltpu.make_async_copy(ready.at[x], out.at[:, x], sems.at[x]))
        moves[-1].start()
    for move in moves:
        move.wait()


def y_edge_kernel(lattice, from_right, from_left, y_offset, y_frac, partial, out, ready, sems):
    width = y_offset.shape[0]
    moves = []
    for number, (x, halo, at) in enumerate(((0, from_left, 0), (1, from_left, 1), (width - 1, from_right, 0))):
        factors = y_factors(y_offset[x], y_frac[x])
        for f in range(FIELDS):
            ready[f, number] = y_spread(lattice[f, x] + halo[f, at], factors)
        moves.append(pltpu.make_async_copy(ready.at[:, number], out.at[:, x], sems.at[number]))
        moves[-1].start()
    for move in moves:
        move.wait()


def params(mib):
    return pltpu.CompilerParams(vmem_limit_bytes=mib << 20)


def bucket(fields, frac, owner, slab, line_in, xcell, count):
    rows = frac.shape[0] // 128
    grid2 = lambda v: v.reshape(rows, 128)
    return pl.pallas_call(
        bucket_kernel,
        out_shape=jax.ShapeDtypeStruct((PEERS, 1, VALUES * SLOTS), F32),
        in_specs=[pl.BlockSpec(memory_space=pltpu.HBM)] * 7,
        scratch_shapes=[
            pltpu.VMEM(fields.shape, F32),
            pltpu.VMEM((rows, 128), F32),
            pltpu.VMEM((rows, 128), jnp.int32),
            pltpu.VMEM((rows, 128), jnp.int32),
            pltpu.VMEM((rows, 128), jnp.int32),
            pltpu.VMEM((rows, 128), jnp.int32),
            pltpu.VMEM((1, rows), jnp.int32),
            pltpu.SemaphoreType.DMA((7,)),
            pltpu.VMEM((rows, 128), F32),
            pltpu.VMEM((rows, 128), F32),
            pltpu.VMEM((4, rows, 128), F32),
            pltpu.VMEM((PEERS, rows * 128), BF16),
            pltpu.VMEM((PEERS, 128), BF16),
            pltpu.VMEM((2 * VALUES * SLOTS, PEERS), F32),
        ],
        compiler_params=params(56),
        name="bucket",
    )(fields, grid2(frac), grid2(owner), grid2(slab), grid2(line_in), grid2(xcell), count.reshape(1, rows))


def deposit(arrived):
    return pl.pallas_call(
        deposit_kernel,
        out_shape=(
            jax.ShapeDtypeStruct((FIELDS, 16, 8, 256), F32),
            jax.ShapeDtypeStruct((FIELDS, 2, 8, 256), F32),
            jax.ShapeDtypeStruct((FIELDS, 2, 8, 256), F32),
        ),
        scratch_shapes=[
            pltpu.VMEM((VALUES * SLOTS, PEERS), F32),
            pltpu.VMEM((SLOTS, PEERS), F32),
            pltpu.VMEM((SLOTS, PEERS), F32),
            pltpu.VMEM((SLOTS, PEERS), F32),
            pltpu.VMEM((PLANES, VALUES, 8, PEERS), F32),
            pltpu.VMEM((PLANES, 4, 8, PEERS), F32),
            pltpu.VMEM((8, 256, 256), F32),
        ],
        compiler_params=params(24),
        name="deposit",
    )(arrived)


def y_inner(lattice, y_offset, y_frac):
    return pl.pallas_call(
        y_inner_kernel,
        out_shape=jax.ShapeDtypeStruct(lattice.shape, F32),
        out_specs=pl.BlockSpec(memory_space=pltpu.HBM),
        scratch_shapes=[
            pltpu.VMEM((lattice.shape[1], FIELDS) + lattice.shape[2:], F32),
            pltpu.SemaphoreType.DMA((lattice.shape[1],)),
        ],
        compiler_params=params(16),
        cost_estimate=pl.CostEstimate(flops=20 * lattice.size, bytes_accessed=8 * lattice.size, transcendentals=0),
        name="y_inner",
    )(lattice, y_offset, y_frac)


def y_edge(lattice, from_right, from_left, y_offset, y_frac, partial):
    vmem = pl.BlockSpec(memory_space=pltpu.VMEM)
    return pl.pallas_call(
        y_edge_kernel,
        out_shape=jax.ShapeDtypeStruct(lattice.shape, F32),
        in_specs=[vmem] * 5 + [pl.BlockSpec(memory_space=pltpu.HBM)],
        out_specs=pl.BlockSpec(memory_space=pltpu.HBM),
        input_output_aliases={5: 0},
        scratch_shapes=[
            pltpu.VMEM((FIELDS, 3) + lattice.shape[2:], F32),
            pltpu.SemaphoreType.DMA((3,)),
        ],
        compiler_params=params(16),
        name="y_edge",
    )(lattice, from_right, from_left, y_offset, y_frac, partial)


def per_device(fields, frac_x, owner, slab, line_in, xcell, tile_count, y_offset, y_frac):
    lines = lax.axis_size("lines")
    outgoing = bucket(fields, frac_x, owner, slab, line_in, xcell, tile_count)
    arrived = lax.all_to_all(outgoing, ("lines", "slab"), split_axis=0, concat_axis=0, tiled=True)
    lattice, low_edge, high_edge = deposit(arrived)
    from_left = lax.ppermute(high_edge, "lines", [(i, (i + 1) % lines) for i in range(lines)])
    from_right = lax.ppermute(low_edge, "lines", [(i, (i - 1) % lines) for i in range(lines)])
    partial = y_inner(lattice, y_offset, y_frac)
    return y_edge(lattice, from_right, from_left, y_offset, y_frac, partial)


def solution(mesh):
    return jax.shard_map(
        per_device,
        mesh=mesh,
        in_specs=(
            P(None, ("lines", "slab")),
            P(("lines", "slab")),
            P(("lines", "slab")),
            P(("lines", "slab")),
            P(("lines", "slab")),
            P(("lines", "slab")),
            P(("lines", "slab")),
            P("lines", "slab", None),
            P("lines", "slab", None),
        ),
        out_specs=P(None, "lines", "slab", None),
        check_vma=False,
    )
```

```python
import functools

import jax
import jax.numpy as jnp
from jax import lax
from jax.experimental import pallas as pl
from jax.experimental.pallas import tpu as pltpu
from jax.sharding import PartitionSpec as P

F32 = jnp.float32
BF16 = jnp.bfloat16
NT = (((1,), (1,)), ((), ()))

FIELDS = 6
SLOTS = 48
VALUES = 8
PEERS = 256
PLANES = 8
OWN = 6


def kernel_weights(offset):
    remain = 1.0 - offset
    return (
        -0.5 * offset * remain * remain,
        1.0 - 2.5 * offset * offset + 1.5 * offset * offset * offset,
        1.0 - 2.5 * remain * remain + 1.5 * remain * remain * remain,
        -0.5 * offset * offset * remain,
    )


def split(value):
    high = value.astype(BF16).astype(F32)
    return high, (value - high).astype(BF16).astype(F32)


def bucket_kernel(
    fields_h, frac_h, owner_h, slab_h, line_in_h, xcell_h, count_h, out,
    fields, frac, owner, slab, line_in, xcell, count, sems, key_s, rank_s, place_s, hot_s, hist_s, acc,
):
    moves = [
        pltpu.make_async_copy(source, goal, sems.at[number])
        for number, (source, goal) in enumerate((
            (count_h, count), (slab_h, slab), (xcell_h, xcell), (owner_h, owner), (line_in_h, line_in), (frac_h, frac),
            (fields_h, fields),
        ))
    ]
    for move in moves:
        move.start()
    for move in moves[:3]:
        move.wait()
    rows = key_s.shape[0]
    lane = lax.broadcasted_iota(jnp.int32, key_s.shape, 1)
    tile = lax.broadcasted_iota(jnp.int32, (rows, rows), 0) == lax.broadcasted_iota(jnp.int32, (rows, rows), 1)
    alive = lane < jnp.sum(jnp.where(tile, count[...], 0), axis=1, keepdims=True)
    key_s[...] = jnp.where(alive, (xcell[...] >> 4) * 8 + slab[...], -1).astype(F32)
    sixteen = lax.broadcasted_iota(jnp.int32, (16, 128), 0).astype(F32)
    one, zero = jnp.ones((), BF16), jnp.zeros((), BF16)

    def wide_row(row):
        return jnp.broadcast_to(row, (16, 128)).astype(BF16)

    total = jnp.zeros((PEERS, 128), BF16)
    for row in range(rows):
        key = wide_row(key_s[row:row + 1, :])
        hot = jnp.concatenate(
            [jnp.where(key == (sixteen + 16.0 * g).astype(BF16), one, zero) for g in range(PEERS // 16)], axis=0
        )
        hot_s[:, row * 128:row * 128 + 128] = hot
        total = total + hot
    earlier = lax.broadcasted_iota(jnp.int32, (128, 128), 0) < lax.broadcasted_iota(jnp.int32, (128, 128), 1)
    base = jnp.dot(total, jnp.where(earlier, 1.0, 0.0).astype(BF16), preferred_element_type=F32)
    hist_s[...] = base.astype(BF16)
    sub = lax.broadcasted_iota(jnp.int32, (8, 128), 0)
    groups = rows // 8
    keys = [key_s[g * 8:g * 8 + 8, :] for g in range(groups)]
    above = [jnp.zeros((8, 128), F32) for _ in range(groups)]
    for row in range(rows):
        key = key_s[row:row + 1, :]
        for g in range(row // 8, groups):
            same = keys[g] == key
            if g == row // 8:
                same = jnp.logical_and(same, sub > row % 8)
            above[g] = above[g] + jnp.where(same, 1.0, 0.0)
    for g in range(groups):
        rank_s[g * 8:g * 8 + 8, :] = above[g]

    for move in moves[3:]:
        move.wait()
    place_s[0] = (owner[...] * 8 + (line_in[...] >> 3)).astype(F32)
    place_s[1] = ((128 + (line_in[...] & 7) * 16 + (xcell[...] & 15)) * 256).astype(F32)
    place_s[2], place_s[3] = split(frac[...])
    wide = 16
    acc[...] = jnp.zeros_like(acc)

    for step in range(rows // wide):
        packed = []
        for part in range(wide):
            row = step * wide + part
            columns = pl.ds(row * 128, 128)
            seen = hot_s[:, columns] * hist_s[...]
            some = seen[0:16]
            for g in range(1, PEERS // 16):
                some = some + seen[g * 16:g * 16 + 16]
            rank = jnp.sum(some.astype(F32), axis=0, keepdims=True) + rank_s[row:row + 1, :]
            rank = wide_row(rank)
            here = [rank == (sixteen + 16.0 * g).astype(BF16) for g in range(SLOTS // 16)]
            high, low = split(fields[:, columns])
            highs = [high[f:f + 1] for f in range(FIELDS)]
            lows = [low[f:f + 1] for f in range(FIELDS)]
            highs += [place_s[2, row:row + 1, :], place_s[0, row:row + 1, :]]
            lows += [place_s[3, row:row + 1, :], place_s[1, row:row + 1, :]]
            pieces = []
            for v in highs + lows:
                v = wide_row(v)
                pieces += [jnp.where(h, v, zero) for h in here]
            packed.append(jnp.concatenate(pieces, axis=0))
        block = hot_s[:, pl.ds(step * wide * 128, wide * 128)]
        acc[...] += lax.dot_general(jnp.concatenate(packed, axis=1), block, NT, preferred_element_type=F32)
    half = VALUES * SLOTS
    total = acc[:half, :] + acc[half:, :]
    out[...] = jnp.swapaxes(total, 0, 1)[:, None, :]


def deposit_kernel(arrived, lattice, low_edge, high_edge, flat_s, plane_s, to_s, over_s, mine_s, weight_s, acc):
    flat_s[...] = jnp.swapaxes(arrived[:, 0, :], 0, 1)
    place = flat_s[7 * SLOTS:8 * SLOTS, :].astype(jnp.int32)
    live = place >= 32768
    plane = jnp.where(live, (place >> 12) & 7, 99).astype(F32)
    plane_s[...] = plane
    sub = lax.broadcasted_iota(jnp.int32, (8, PEERS), 0)
    subf = sub.astype(F32)
    seen = jnp.zeros((PLANES, PEERS), F32)
    for slot in range(SLOTS):
        hit = plane_s[slot:slot + 1, :] == subf
        to_s[slot:slot + 1, :] = jnp.sum(jnp.where(hit, seen, 0.0), axis=0, keepdims=True)
        seen = seen + jnp.where(hit, 1.0, 0.0)
    rank = to_s[...]
    fits = rank < OWN
    to_s[...] = jnp.where(fits, plane * 8 + rank, 9999.0)
    extra = jnp.logical_and(live, jnp.logical_not(fits))
    before = lax.broadcasted_iota(jnp.int32, (SLOTS, SLOTS), 1) < lax.broadcasted_iota(jnp.int32, (SLOTS, SLOTS), 0)
    order = jnp.dot(jnp.where(before, 1.0, 0.0).astype(BF16), jnp.where(extra, 1.0, 0.0).astype(BF16), preferred_element_type=F32)
    over_s[...] = jnp.where(extra, order, -1.0)
    left = jnp.sum(jnp.maximum(seen - OWN, 0.0), axis=0, keepdims=True)
    most = jnp.max(left, axis=1, keepdims=True)
    tiled = jnp.minimum(left, 16.0)
    few = jnp.sum(tiled, axis=1, keepdims=True) <= PEERS
    first_round = jnp.max(jnp.where(few, 16.0, 0.0)).astype(jnp.int32)
    last_round = jnp.max(most).astype(jnp.int32)

    low_rows = (sub + 1).astype(F32)
    high_rows = (sub + 9).astype(F32)
    edge_rows = jnp.where(sub % 4 == 0, 0, jnp.where(sub % 4 == 3, 99, 16 + sub % 4)).astype(F32)
    first = sub < 4
    sixteen = lax.broadcasted_iota(jnp.int32, (16, PEERS), 0).astype(F32)
    levels = [(sixteen + 16.0 * g).astype(BF16) for g in range(16)]

    one, zero = jnp.ones((), BF16), jnp.zeros((), BF16)

    def hot(row):
        row = jnp.broadcast_to(row, (16, PEERS)).astype(BF16)
        return jnp.concatenate([jnp.where(row == level, one, zero) for level in levels], axis=0)

    def rows_of(weights, xin, field):
        spread = []
        for nodes, reach in ((low_rows, range(4)), (high_rows, range(4)), (edge_rows, (0, 2, 3))):
            apart = nodes - xin
            value = jnp.zeros((8, PEERS), F32)
            for k in reach:
                value = jnp.where(apart == float(k), weights[k], value)
            spread.append(value)
        groups = []
        for f in range(FIELDS):
            groups += [spread[0] * field[f], spread[1] * field[f]]
        for f in range(0, FIELDS, 2):
            groups.append(spread[2] * jnp.where(first, field[f], field[f + 1]))
        groups.append(jnp.zeros((8, PEERS), F32))
        whole = jnp.concatenate(groups, axis=0)
        high = whole.astype(BF16)
        low = (whole - high.astype(F32)).astype(BF16)
        return jnp.concatenate([high, low], axis=0)

    def gather(goals):
        found = [[jnp.zeros((8, PEERS), F32) for _ in range(VALUES)] for _ in goals]
        for slot in range(SLOTS):
            rows = [flat_s[v * SLOTS + slot:v * SLOTS + slot + 1, :] for v in range(VALUES)]
            for part, (numbers, goal) in enumerate(goals):
                hit = numbers[slot:slot + 1, :] == goal
                found[part] = [jnp.where(hit, rows[v], found[part][v]) for v in range(VALUES)]
        return found

    stacks = []
    for found in gather([(over_s, subf), (over_s, subf + 8.0)]):
        pieces = [split(v) for v in found]
        stacks.append(jnp.concatenate([p[0] for p in pieces] + [p[1] for p in pieces], axis=0).astype(BF16))
    lanes = lax.broadcasted_iota(jnp.int32, (PEERS, PEERS), 0)
    ahead = jnp.where(lanes < lax.broadcasted_iota(jnp.int32, (PEERS, PEERS), 1), 1.0, 0.0).astype(BF16)
    start = jnp.dot(jnp.broadcast_to(tiled, (16, PEERS)).astype(BF16), ahead, preferred_element_type=F32)[0:1]
    picked = [jnp.zeros((8, PEERS), F32) for _ in range(VALUES)]
    for k in range(16):
        spot = jnp.where(jnp.logical_and(left > k, few), start + k, -1.0)
        moved = lax.dot_general(stacks[k // 8], hot(spot), NT, preferred_element_type=F32)
        for v in range(VALUES):
            value = moved[v * 8:v * 8 + 8] + moved[(VALUES + v) * 8:(VALUES + v) * 8 + 8]
            picked[v] = picked[v] + jnp.where(sub == k % 8, value, 0.0)
    picked = [jnp.sum(v, axis=0, keepdims=True) for v in picked]
    spot = picked[7].astype(jnp.int32)
    few_rows = rows_of(kernel_weights(picked[6]), ((spot >> 8) & 15).astype(F32), picked[:FIELDS])
    few_plane = (spot >> 12) & 7
    few_y = (spot & 255).astype(F32)

    pair = 1
    for step in range(PLANES // pair):
        found = gather([(to_s, subf + float((step * pair + part) * 8)) for part in range(pair)])
        for part in range(pair):
            spot = found[part][7].astype(jnp.int32)
            z = step * pair + part
            for v in range(FIELDS):
                mine_s[z, v] = found[part][v]
            mine_s[z, 6] = ((spot >> 8) & 15).astype(F32)
            mine_s[z, 7] = (spot & 255).astype(F32)
            for number, weight in enumerate(kernel_weights(found[part][6])):
                weight_s[z, number] = weight
    for z in range(PLANES):
        packed, ones = [few_rows], [hot(jnp.where(few_plane == z, few_y, -1.0))]
        for own in range(OWN):
            row = lambda v: mine_s[z, v, own:own + 1, :]
            packed.append(rows_of([weight_s[z, k, own:own + 1, :] for k in range(4)], row(6), [row(f) for f in range(FIELDS)]))
            ones.append(hot(row(7)))
        acc[z] = lax.dot_general(
            jnp.concatenate(ones, axis=1), jnp.concatenate(packed, axis=1), NT, preferred_element_type=F32
        )

    def extra_step(number, carry):
        hit = over_s[...] == number.astype(F32)
        pick = lambda v: jnp.sum(jnp.where(hit, flat_s[v * SLOTS:(v + 1) * SLOTS, :], 0.0), axis=0, keepdims=True)
        field = [pick(f) for f in range(FIELDS)]
        weights = kernel_weights(pick(6))
        spot = pick(7).astype(jnp.int32)
        packed = rows_of(weights, ((spot >> 8) & 15).astype(F32), field)
        plane = (spot >> 12) & 7
        spot_y = (spot & 255).astype(F32)
        for z in range(PLANES):
            acc[z] += lax.dot_general(hot(jnp.where(plane == z, spot_y, -1.0)), packed, NT, preferred_element_type=F32)
        return carry

    lax.fori_loop(first_round, last_round, extra_step, 0)
    low_edge[:, 1] = jnp.zeros((FIELDS,) + low_edge.shape[2:], F32)
    for z in range(PLANES):
        nodes = jnp.swapaxes(acc[z, :, :128] + acc[z, :, 128:], 0, 1)
        for f in range(FIELDS):
            for half in range(2):
                at = (f * 2 + half) * 8
                lattice[f, half * 8:half * 8 + 8, z, :] = nodes[at:at + 8, :]
            at = 96 + f * 4
            low_edge[f, 0, z:z + 1, :] = nodes[at:at + 1, :]
            high_edge[f, 0, z:z + 1, :] = nodes[at + 1:at + 2, :]
            high_edge[f, 1, z:z + 1, :] = nodes[at + 2:at + 3, :]


def y_factors(y_offset, y_frac):
    weights = kernel_weights(y_frac)
    is_shift = [y_offset == s for s in range(-2, 3)]
    factors = []
    for travel in range(-3, 5):
        factor = jnp.zeros_like(weights[0])
        for s in range(-2, 3):
            if -1 <= travel - s <= 2:
                factor = jnp.where(is_shift[s + 2], weights[travel - s + 1], factor)
        factors.append(factor)
    return factors


def y_spread(values, factors):
    total = values * factors[3]
    for travel in range(-3, 5):
        if travel:
            total = total + pltpu.roll(values * factors[travel + 3], travel % values.shape[1], 1)
    return total


def y_inner_kernel(lattice, y_offset, y_frac, out, ready, sems):
    width = y_offset.shape[0]

    moves = []
    for x in range(2, width - 1):
        factors = y_factors(y_offset[x], y_frac[x])
        for f in range(FIELDS):
            ready[x, f] = y_spread(lattice[f, x], factors)
        moves.append(pltpu.make_async_copy(ready.at[x], out.at[:, x], sems.at[x]))
        moves[-1].start()
    for move in moves:
        move.wait()


def y_edge_kernel(lattice, from_right, from_left, y_offset, y_frac, partial, out, ready, sems):
    width = y_offset.shape[0]
    moves = []
    for number, (x, halo, at) in enumerate(((0, from_left, 0), (1, from_left, 1), (width - 1, from_right, 0))):
        factors = y_factors(y_offset[x], y_frac[x])
        for f in range(FIELDS):
            ready[f, number] = y_spread(lattice[f, x] + halo[f, at], factors)
        moves.append(pltpu.make_async_copy(ready.at[:, number], out.at[:, x], sems.at[number]))
        moves[-1].start()
    for move in moves:
        move.wait()


def params(mib):
    return pltpu.CompilerParams(vmem_limit_bytes=mib << 20)


def bucket(fields, frac, owner, slab, line_in, xcell, count):
    rows = frac.shape[0] // 128
    grid2 = lambda v: v.reshape(rows, 128)
    return pl.pallas_call(
        bucket_kernel,
        out_shape=jax.ShapeDtypeStruct((PEERS, 1, VALUES * SLOTS), F32),
        in_specs=[pl.BlockSpec(memory_space=pltpu.HBM)] * 7,
        scratch_shapes=[
            pltpu.VMEM(fields.shape, F32),
            pltpu.VMEM((rows, 128), F32),
            pltpu.VMEM((rows, 128), jnp.int32),
            pltpu.VMEM((rows, 128), jnp.int32),
            pltpu.VMEM((rows, 128), jnp.int32),
            pltpu.VMEM((rows, 128), jnp.int32),
            pltpu.VMEM((1, rows), jnp.int32),
            pltpu.SemaphoreType.DMA((7,)),
            pltpu.VMEM((rows, 128), F32),
            pltpu.VMEM((rows, 128), F32),
            pltpu.VMEM((4, rows, 128), F32),
            pltpu.VMEM((PEERS, rows * 128), BF16),
            pltpu.VMEM((PEERS, 128), BF16),
            pltpu.VMEM((2 * VALUES * SLOTS, PEERS), F32),
        ],
        compiler_params=params(56),
        name="bucket",
    )(fields, grid2(frac), grid2(owner), grid2(slab), grid2(line_in), grid2(xcell), count.reshape(1, rows))


def deposit(arrived):
    return pl.pallas_call(
        deposit_kernel,
        out_shape=(
            jax.ShapeDtypeStruct((FIELDS, 16, 8, 256), F32),
            jax.ShapeDtypeStruct((FIELDS, 2, 8, 256), F32),
            jax.ShapeDtypeStruct((FIELDS, 2, 8, 256), F32),
        ),
        scratch_shapes=[
            pltpu.VMEM((VALUES * SLOTS, PEERS), F32),
            pltpu.VMEM((SLOTS, PEERS), F32),
            pltpu.VMEM((SLOTS, PEERS), F32),
            pltpu.VMEM((SLOTS, PEERS), F32),
            pltpu.VMEM((PLANES, VALUES, 8, PEERS), F32),
            pltpu.VMEM((PLANES, 4, 8, PEERS), F32),
            pltpu.VMEM((8, 256, 256), F32),
        ],
        compiler_params=params(24),
        name="deposit",
    )(arrived)


def y_inner(lattice, y_offset, y_frac):
    return pl.pallas_call(
        y_inner_kernel,
        out_shape=jax.ShapeDtypeStruct(lattice.shape, F32),
        out_specs=pl.BlockSpec(memory_space=pltpu.HBM),
        scratch_shapes=[
            pltpu.VMEM((lattice.shape[1], FIELDS) + lattice.shape[2:], F32),
            pltpu.SemaphoreType.DMA((lattice.shape[1],)),
        ],
        compiler_params=params(16),
        cost_estimate=pl.CostEstimate(flops=20 * lattice.size, bytes_accessed=8 * lattice.size, transcendentals=0),
        name="y_inner",
    )(lattice, y_offset, y_frac)


def y_edge(lattice, from_right, from_left, y_offset, y_frac, partial):
    vmem = pl.BlockSpec(memory_space=pltpu.VMEM)
    return pl.pallas_call(
        y_edge_kernel,
        out_shape=jax.ShapeDtypeStruct(lattice.shape, F32),
        in_specs=[vmem] * 5 + [pl.BlockSpec(memory_space=pltpu.HBM)],
        out_specs=pl.BlockSpec(memory_space=pltpu.HBM),
        input_output_aliases={5: 0},
        scratch_shapes=[
            pltpu.VMEM((FIELDS, 3) + lattice.shape[2:], F32),
            pltpu.SemaphoreType.DMA((3,)),
        ],
        compiler_params=params(16),
        name="y_edge",
    )(lattice, from_right, from_left, y_offset, y_frac, partial)


def per_device(fields, frac_x, owner, slab, line_in, xcell, tile_count, y_offset, y_frac):
    lines = lax.axis_size("lines")
    outgoing = bucket(fields, frac_x, owner, slab, line_in, xcell, tile_count)
    arrived = lax.all_to_all(outgoing, ("lines", "slab"), split_axis=0, concat_axis=0, tiled=True)
    lattice, low_edge, high_edge = deposit(arrived)
    from_left = lax.ppermute(high_edge, "lines", [(i, (i + 1) % lines) for i in range(lines)])
    from_right = lax.ppermute(low_edge, "lines", [(i, (i - 1) % lines) for i in range(lines)])
    partial = y_inner(lattice, y_offset, y_frac)
    return y_edge(lattice, from_right, from_left, y_offset, y_frac, partial)


def solution(mesh):
    return jax.shard_map(
        per_device,
        mesh=mesh,
        in_specs=(
            P(None, ("lines", "slab")),
            P(("lines", "slab")),
            P(("lines", "slab")),
            P(("lines", "slab")),
            P(("lines", "slab")),
            P(("lines", "slab")),
            P(("lines", "slab")),
            P("lines", "slab", None),
            P("lines", "slab", None),
        ),
        out_specs=P(None, "lines", "slab", None),
        check_vma=False,
    )
```
